32 devices in a mesh: seg: 2 (over x), ctx: 16 (over z, y, core).
Axes of the slice: x: 2, y: 2, z: 4, core: 2. Of those that a mesh axis runs over, the one named last changes fastest.
Arguments:
- hidden_in: bfloat16 [4096, 1024], P(('seg', 'ctx')), may hold values from -6 to 6
- queries: bfloat16 [4096, 1024], P(('seg', 'ctx')), may hold values from -6 to 6
- key_rows: bfloat16 [4096, 1024], P(('seg', 'ctx')), may hold values from -6 to 6
- values: bfloat16 [4096, 1024], P(('seg', 'ctx')), may hold values from -6 to 6
- norm_gain: float32 [1024], replicated, may hold values from 0.5 to 1.5
- out_proj: bfloat16 [1024, 1024], replicated, may hold values from -0.1875 to 0.1875
- moe_gain: float32 [1024], replicated, may hold values from 0.5 to 1.5
- w_gate: bfloat16 [16, 1024, 896], P('ctx'), may hold values from -0.1875 to 0.1875
- w_up: bfloat16 [16, 1024, 896], P('ctx'), may hold values from -0.1875 to 0.1875
- w_down: bfloat16 [16, 896, 1024], P('ctx'), may hold values from -0.1875 to 0.1875
- expert_ids: int32 [4096, 8], P(('seg', 'ctx')), may hold values from 0 to 15, all different within a row; in each aligned block of 128 rows (0 to 127, 128 to 255, ...) at most 96 rows name the same one
- route_scale: int32 [4096, 8], P(('seg', 'ctx')), may hold values from 1 to 4095
Outputs:
- layer_out: bfloat16 [4096, 1024], P(('seg', 'ctx'))
The draws below stay inside these ranges and needn't reach their ends.
Inputs may be any that keep to these rules, and one draw needn't show every extreme that they name: `expert_ids`: each row names 8 different experts. Among the rows of one device no expert is named more than 96 times, and in every draw some device names some expert exactly 96 times.
All inputs are finite; a program needn't handle non-finite values.
Results may differ from the reference program's by a relative error of at most 0.0075.
Values may be sent and summed in bfloat16 or wider, within the bound.
No kernel may reach another device: no remote copies, remote signals or barrier semaphores. Data moves between devices by JAX's collectives and lax.ppermute only.
A program may use at most 192 MiB of HBM per device.

```python
import math
import jax
import jax.numpy as jnp
import numpy as np
from jax import lax

HEADS = 8
HEAD = 128
D = 1024
FF = 896
TOP = 8
TOK_DEV = 128
EXPERTS = 16
TOKENS = 4096
CAP = 96


def touch_ends(values, own_key, least, high):
    extent = values.shape
    spot = [jax.random.randint(jax.random.fold_in(own_key, axis), (), 0, extent[axis]) for axis in range(len(extent))]
    values = values.at[tuple(spot)].set(least)
    longest = extent.index(max(extent))
    spot[longest] = (spot[longest] + 1) % extent[longest]
    return values.at[tuple(spot)].set(high)


def levels(own_key, dims, shards, least, top_value):
    def one(position, shards_of):
        steps = jax.random.uniform(jax.random.fold_in(jax.random.fold_in(own_key, 6), position), (shards_of,), jnp.float32, least / len(shards), top_value / len(shards))
        return jnp.repeat(jnp.exp(steps), dims[position] // shards_of).reshape((-1,) + (1,) * (len(dims) - position - 1))

    loudness = one(*shards[0])
    for cut in shards[1:]:
        loudness = loudness * one(*cut)
    return loudness


def shared_out(key, own, number, rows, amount, top, limit, lean):
    order = jax.random.permutation(key, amount)
    packed, usual = load_shares(amount, rows * top, limit, lean, True), load_shares(amount, rows * top, limit, lean, False)
    places = jnp.arange(amount)

    def named(sizes, rotation):
        used = int((sizes > 0).sum())
        fixed = max(1, used // 4)
        passed = fixed + (places - fixed + rotation * (used - fixed)) % max(1, amount - fixed)
        return jnp.zeros((amount,), jnp.int32).at[order[jnp.where(places < fixed, places, passed)]].set(jnp.asarray(sizes, jnp.int32))

    sizes = jnp.where(number % 4 == 0, named(packed, number // 4), named(usual, number - number // 4 - 1))
    mixed = jax.random.permutation(jax.random.fold_in(own, 3), amount)
    donor, sink = mixed[0:amount // 2 * 2:2], mixed[1:amount // 2 * 2:2]
    room = jnp.minimum(sizes[donor] - 1, limit - sizes[sink]) // 2
    room = jnp.where((donor == order[0]) | (sink == order[0]) | (sizes[sink] == 0), 0, jnp.maximum(room, 0))
    passed = jax.random.randint(jax.random.fold_in(own, 4), (amount // 2,), 0, 1 << 20) % (room + 1)
    sizes = sizes.at[donor].add(-passed).at[sink].add(passed)
    items = jnp.searchsorted(jnp.cumsum(sizes), jnp.arange(rows * top), side="right").astype(jnp.int32)
    grid = items.reshape(top, rows).T
    grid = grid[jax.random.permutation(jax.random.fold_in(own, 1), rows)]
    rotation = jax.random.randint(jax.random.fold_in(own, 2), (rows, 1), 0, top)
    return jnp.take_along_axis(grid, (jnp.arange(top)[None, :] + rotation) % top, axis=1)


def load_shares(amount, total, most, skew, full):
    portions = [(1 << 20) // math.isqrt(rank ** skew) + 1 for rank in range(1, amount + 1)]
    largest = most if full else min(most, max(-(-total // amount), total * portions[0] // sum(portions)))
    least = 1 if total - largest >= amount - 1 else 0
    given, rest = [largest] + [least] * (amount - 1), total - largest - least * (amount - 1)
    while rest > 0:
        candidates = [i for i in range(1, amount) if given[i] < largest] or [i for i in range(1, amount) if given[i] < most]
        mass, remaining = sum([portions[i] for i in candidates]), rest
        for i in candidates:
            extra = min(most - given[i], max(1, remaining * portions[i] // mass), rest)
            given[i] = given[i] + extra
            rest = rest - extra
    return np.array(given)


def scatter_about(own_key, shape, scale, reach, split=(), kind=jnp.bfloat16):
    array = scale * jax.random.normal(own_key, shape, jnp.float32)
    if split:
        array = array * levels(own_key, shape, split, -0.22, 0.18)
    return jnp.clip(array, -reach, reach).astype(kind)


def setup_inputs(seed: int = 0) -> dict:
    splits = jax.random.split(jax.random.key(seed), 13)
    hidden_in = scatter_about(splits[0], (TOKENS, D), 1.0, 6.0, ((0, 32),))
    queries = scatter_about(splits[1], (TOKENS, D), 1.0, 6.0, ((0, 32),))
    key_rows = scatter_about(splits[2], (TOKENS, D), 1.0, 6.0, ((0, 32),))
    values = scatter_about(splits[3], (TOKENS, D), 1.0, 6.0, ((0, 32),))
    norm_gain = jnp.clip(1.0 + 0.1 * jax.random.normal(splits[4], (D,), jnp.float32), 0.5, 1.5)
    out_proj = scatter_about(splits[5], (D, D), D ** -0.5, 0.1875)
    moe_gain = jnp.clip(1.0 + 0.1 * jax.random.normal(splits[6], (D,), jnp.float32), 0.5, 1.5)
    w_gate = scatter_about(splits[7], (EXPERTS, D, FF), D ** -0.5, 0.1875, ((0, 16),))
    w_up = scatter_about(splits[8], (EXPERTS, D, FF), D ** -0.5, 0.1875, ((0, 16),))
    w_down = scatter_about(splits[9], (EXPERTS, FF, D), FF ** -0.5, 0.1875, ((0, 16),))
    expert_ids_keys = jax.random.split(jax.random.fold_in(splits[10], 1), TOKENS // TOK_DEV)
    expert_ids_turns = jax.random.permutation(jax.random.fold_in(splits[10], 3), TOKENS // TOK_DEV)
    expert_ids = jax.vmap(lambda own, number: shared_out(jax.random.fold_in(splits[10], 2), own, number, TOK_DEV, EXPERTS, TOP, CAP, 1))(expert_ids_keys, expert_ids_turns).reshape((TOKENS, TOP))
    route_scale = touch_ends(jax.random.randint(splits[11], (TOKENS, TOP), 1, 4096), jax.random.fold_in(splits[11], 1), 1, 4095).astype(jnp.int32)
    return dict(hidden_in=hidden_in, queries=queries, key_rows=key_rows, values=values, norm_gain=norm_gain, out_proj=out_proj, moe_gain=moe_gain, w_gate=w_gate, w_up=w_up, w_down=w_down, expert_ids=expert_ids, route_scale=route_scale)


def attention_all(queries, key_rows, values):
    width = math.gcd(512, TOKENS)
    count = TOKENS // width
    q_all = queries.astype(jnp.float32).reshape(count, width, HEADS, HEAD)
    k_all = key_rows.astype(jnp.float32).reshape(count, width, HEADS, HEAD)
    v_all = values.astype(jnp.float32).reshape(count, width, HEADS, HEAD)
    causal = jnp.arange(width)[:, None] >= jnp.arange(width)[None, :]
    high = lax.Precision.HIGHEST

    def stepper(states, item):
        q_blk, k_blk, v_blk = item
        carried = jnp.einsum('thd,hde->the', q_blk, states, precision=high)
        scores = jnp.einsum('thd,shd->hts', q_blk, k_blk, precision=high)
        scores = jnp.where(causal[None, :, :], scores, jnp.zeros((), jnp.float32))
        inside = jnp.einsum('hts,she->the', scores, v_blk, precision=high)
        states = states + jnp.einsum('thd,the->hde', k_blk, v_blk, precision=high)
        return (states, carried + inside)
    start = jnp.zeros((HEADS, HEAD, HEAD), jnp.float32)
    final, outputs = lax.scan(stepper, start, (q_all, k_all, v_all))
    return outputs.reshape(TOKENS, D)

def rms_scale(rows, gain):
    mean_sq = lax.optimization_barrier(jnp.mean(rows * rows, axis=1, keepdims=True))
    return rows * lax.rsqrt(mean_sq + 1e-06) * gain[None, :]

def reference(hidden_in, queries, key_rows, values, norm_gain, out_proj, moe_gain, w_gate, w_up, w_down, expert_ids, route_scale):
    attended = attention_all(queries, key_rows, values)
    normed = rms_scale(attended, norm_gain).astype(jnp.bfloat16)
    mixed = hidden_in.astype(jnp.float32) + jnp.dot(normed, out_proj, preferred_element_type=jnp.float32)
    routed = rms_scale(mixed, moe_gain).astype(jnp.bfloat16)
    scales = route_scale.astype(jnp.float32)
    weight = (scales / lax.optimization_barrier(jnp.sum(scales, axis=1, keepdims=True))).reshape(-1)
    blocksz = 512
    flat = expert_ids.reshape(-1).astype(jnp.int32)
    npairs = flat.shape[0]
    order = jnp.argsort(flat, stable=True).astype(jnp.int32)
    counts = lax.optimization_barrier(jnp.sum((flat[:, None] == jnp.arange(EXPERTS, dtype=jnp.int32)[None, :]).astype(jnp.int32), axis=0))
    padded = (counts + blocksz - 1) // blocksz * blocksz
    pstart = jnp.cumsum(padded) - padded
    cstart = jnp.cumsum(counts) - counts
    sorted_exp = flat[order]
    ranked = jnp.arange(npairs, dtype=jnp.int32) - cstart[sorted_exp]
    dest = (pstart[sorted_exp] + ranked).astype(jnp.int32)
    nblocks = npairs // blocksz + EXPERTS
    table = jnp.full((nblocks * blocksz,), -1, jnp.int32).at[dest].set(order).reshape(nblocks, blocksz)
    pend = pstart + padded
    starts = jnp.arange(nblocks, dtype=jnp.int32) * blocksz
    owner = jnp.minimum(lax.optimization_barrier(jnp.sum((pend[None, :] <= starts[:, None]).astype(jnp.int32), axis=1)), EXPERTS - 1).astype(jnp.int32)

    def expert_step(accum, item):
        members, expert = item
        valid = members >= 0
        member = jnp.maximum(members, 0)
        token_of = member // TOP
        rows = routed[token_of].astype(jnp.float32)
        gate = jnp.dot(rows, w_gate[expert].astype(jnp.float32))
        upper = jnp.dot(rows, w_up[expert].astype(jnp.float32))
        inner = lax.optimization_barrier((jax.nn.silu(gate) * upper).astype(jnp.bfloat16)).astype(jnp.float32)
        result = lax.optimization_barrier(jnp.dot(inner, w_down[expert].astype(jnp.float32)).astype(jnp.bfloat16)).astype(jnp.float32)
        factor = jnp.where(valid, weight[member], jnp.zeros((), jnp.float32))
        accum = accum.at[token_of].add(factor[:, None] * result)
        return (accum, None)
    total, unused = lax.scan(expert_step, mixed, (table, owner))
    return total.astype(jnp.bfloat16)
```

```python
import functools

import jax
import jax.numpy as jnp
from jax import lax
from jax.experimental import pallas as pl
from jax.experimental.pallas import tpu as pltpu
from jax.sharding import PartitionSpec as P

HEADS = 8
HEAD = 128
BOTH = ("seg", "ctx")
F32 = jnp.float32
BF16 = jnp.bfloat16


def rms_scale(rows, gain):
    mean_sq = jnp.mean(rows * rows, axis=1, keepdims=True)
    return rows * lax.rsqrt(mean_sq + 1e-06) * gain[None, :]


def chip_order(chips):
    return list(range(0, chips, 2)) + list(range(1, chips, 2))[::-1]


def ring_perm(chips, shift):
    order = chip_order(chips)
    pairs = []
    for place, chip in enumerate(order):
        target = order[(place + shift) % chips]
        pairs += [(chip * 2 + core, target * 2 + core) for core in range(2)]
    return pairs


def core_perm(chips):
    return [(dev, dev ^ 1) for dev in range(2 * chips)]


def scan_and_weights(own_state, dense):
    heads, rows, cols = own_state.shape
    ntok, owners = dense.shape
    segs, devices = lax.axis_size("seg"), lax.axis_size(BOTH)
    share = heads * rows // devices
    top = dense.astype(BF16)
    rest = (dense - top.astype(F32)).astype(BF16)
    split = jnp.stack([top.T, rest.T], axis=1).reshape(owners, 2 * ntok // cols, cols)
    split = jnp.broadcast_to(split[None], (segs,) + split.shape).reshape((devices,) + split.shape[1:])
    pieces = own_state.astype(BF16).reshape(devices, share, cols)
    pieces = jnp.concatenate([pieces, split], axis=1)
    pieces = lax.all_to_all(pieces, BOTH, split_axis=0, concat_axis=0, tiled=True)
    split = lax.dynamic_slice_in_dim(pieces[:, share:], lax.axis_index("seg") * owners, owners)
    split = split.reshape(owners, 2, ntok).astype(F32)
    mine = (split[:, 0] + split[:, 1]).T
    earlier = jnp.arange(devices)[:, None] > jnp.arange(devices)[None, :]
    sums = jnp.dot(
        earlier.astype(BF16),
        pieces[:, :share].reshape(devices, share * cols),
        preferred_element_type=F32,
    )
    sums = sums.astype(BF16).reshape(devices, share, cols)
    sums = lax.all_to_all(sums, BOTH, split_axis=0, concat_axis=0, tiled=True)
    return sums.reshape(heads, rows, cols), mine


def expert_kernel(count, sources, dense, w_gate, w_up, w_down, *refs):
    ntok = refs[0].shape[0]
    rows = jnp.concatenate([refs[i][...] for i in range(count)])
    gate = jnp.dot(rows, w_gate[0], preferred_element_type=F32)
    upper = jnp.dot(rows, w_up[0], preferred_element_type=F32)
    inner = (gate / (1.0 + jnp.exp(-gate)) * upper).astype(BF16)
    result = jnp.dot(inner, w_down[0], preferred_element_type=F32)
    table = dense[...]
    lane = lax.broadcasted_iota(jnp.int32, table.shape, 1)
    for i in range(count):
        picked = jnp.where(lane == sources[i], table, 0.0)
        scale = jnp.sum(picked, axis=1, keepdims=True)
        refs[count + i][...] = (result[i * ntok : (i + 1) * ntok] * scale).astype(BF16)


def expert(shards, sources, dense, w_gate, w_up, w_down):
    count, (ntok, width) = len(shards), shards[0].shape
    whole = pl.BlockSpec(memory_space=pltpu.VMEM)
    hidden = w_gate.shape[2]
    return pl.pallas_call(
        functools.partial(expert_kernel, count),
        out_shape=[jax.ShapeDtypeStruct((ntok, width), BF16)] * count,
        in_specs=[pl.BlockSpec(memory_space=pltpu.SMEM)] + [whole] * (4 + count),
        out_specs=[whole] * count,
        compiler_params=pltpu.CompilerParams(vmem_limit_bytes=32 * 1024 * 1024),
        cost_estimate=pl.CostEstimate(
            flops=6 * count * ntok * width * hidden, bytes_accessed=0, transcendentals=0
        ),
    )(jnp.stack(sources), dense, w_gate, w_up, w_down, *shards)


def body(
    hidden_in,
    queries,
    key_rows,
    values,
    norm_gain,
    out_proj,
    moe_gain,
    w_gate,
    w_up,
    w_down,
    expert_ids,
    route_scale,
):
    ntok, width = queries.shape
    owners = lax.axis_size("ctx")
    chips = owners // 2
    me = lax.axis_index("ctx")

    scales = route_scale.astype(F32)
    weight = scales / jnp.sum(scales, axis=1, keepdims=True)
    grid = jnp.arange(owners, dtype=jnp.int32)
    dense = jnp.sum(
        jnp.where(expert_ids[:, :, None] == grid[None, None, :], weight[:, :, None], 0.0), axis=1
    )

    q_loc = queries.reshape(ntok, HEADS, HEAD)
    k_loc = key_rows.reshape(ntok, HEADS, HEAD)
    v_loc = values.reshape(ntok, HEADS, HEAD)
    own_state = jnp.einsum("thd,the->hde", k_loc, v_loc, preferred_element_type=F32)
    earlier, mine_dense = scan_and_weights(own_state, dense)
    causal = jnp.arange(ntok)[:, None] >= jnp.arange(ntok)[None, :]
    scores = jnp.einsum("thd,shd->hts", q_loc, k_loc, preferred_element_type=F32)
    scores = jnp.where(causal[None, :, :], scores, 0.0).astype(BF16)
    inside = jnp.einsum("hts,she->the", scores, v_loc, preferred_element_type=F32)
    carried = jnp.einsum("thd,hde->the", q_loc, earlier, preferred_element_type=F32)
    attended = (carried + inside).reshape(ntok, width)
    normed = rms_scale(attended, norm_gain).astype(BF16)
    mixed = hidden_in.astype(F32) + jnp.dot(normed, out_proj, preferred_element_type=F32)
    routed = rms_scale(mixed, moe_gain).astype(BF16)

    half = chips // 2
    cut = ntok // 2
    order = chip_order(chips)
    place_of = [order.index(chip) for chip in range(chips)]
    place = jnp.asarray(place_of, jnp.int32)[me // 2]
    up, down, swap = ring_perm(chips, 1), ring_perm(chips, -1), core_perm(chips)

    from_below, from_above = [routed], [routed]
    for step in range(1, half):
        from_below.append(lax.ppermute(from_below[-1], "ctx", up))
        from_above.append(lax.ppermute(from_above[-1], "ctx", down))
    far = jnp.concatenate(
        [
            lax.ppermute(from_below[-1][:cut], "ctx", up),
            lax.ppermute(from_above[-1][cut:], "ctx", down),
        ]
    )
    shards = {0: routed, half: far}
    for step in range(1, half):
        shards[-step] = from_below[step]
        shards[step] = from_above[step]

    parts = {}
    for step in range(half + 1):
        offsets = [step] if step in (0, half) else [step, -step]
        group, sources = [], []
        for offset in offsets:
            chip = jnp.asarray(order, jnp.int32)[(place + offset) % chips]
            source = chip * 2 + me % 2
            group += [shards[offset], lax.ppermute(shards[offset], "ctx", swap)]
            sources += [source, source ^ 1]
        results = expert(group, sources, mine_dense, w_gate, w_up, w_down)
        for i, offset in enumerate(offsets):
            partner = lax.ppermute(results[2 * i + 1], "ctx", swap)
            parts[offset] = results[2 * i].astype(F32) + partner.astype(F32)

    far = parts[half].astype(BF16)
    going_up = lax.ppermute(far[:cut], "ctx", up).astype(F32)
    going_down = lax.ppermute(far[cut:], "ctx", down).astype(F32)
    blank = jnp.zeros((ntok - cut, width), F32)
    going_up = jnp.concatenate([going_up, blank])
    going_down = jnp.concatenate([blank[:cut], going_down])
    for step in range(half - 1, 0, -1):
        going_up = lax.ppermute((parts[step] + going_up).astype(BF16), "ctx", up).astype(F32)
        going_down = lax.ppermute((parts[-step] + going_down).astype(BF16), "ctx", down).astype(F32)
    return (mixed + parts[0] + going_up + going_down).astype(BF16)


def solution(mesh):
    rows = P(BOTH, None)
    expert_spec = P("ctx", None, None)
    return jax.shard_map(
        body,
        mesh=mesh,
        in_specs=(rows,) * 4 + (P(),) * 3 + (expert_spec,) * 3 + (rows,) * 2,
        out_specs=rows,
        check_vma=False,
    )
```

```python
import functools

import jax
import jax.numpy as jnp
from jax import lax
from jax.experimental import pallas as pl
from jax.experimental.pallas import tpu as pltpu
from jax.sharding import PartitionSpec as P

HEADS = 8
HEAD = 128
HALVES = 2
BOTH = ("seg", "ctx")
F32 = jnp.float32
BF16 = jnp.bfloat16
VMEM = pl.BlockSpec(memory_space=pltpu.VMEM)
HBM = pl.BlockSpec(memory_space=pltpu.HBM)
LIMIT = 16 * 1024 * 1024


def call(kernel, out_shape, in_specs, flops, *operands):
    many = isinstance(out_shape, list)
    return pl.pallas_call(
        kernel,
        out_shape=out_shape,
        in_specs=in_specs,
        out_specs=[VMEM] * len(out_shape) if many else VMEM,
        compiler_params=pltpu.CompilerParams(vmem_limit_bytes=LIMIT),
        cost_estimate=pl.CostEstimate(flops=flops, bytes_accessed=0, transcendentals=0),
    )(*operands)


def in_hbm(array):
    return pltpu.with_memory_space_constraint(array, pltpu.HBM)


def copies_of(sources, targets, sems):
    copies = [
        pltpu.make_async_copy(source, target, sems.at[i])
        for i, (source, target) in enumerate(zip(sources, targets))
    ]
    for copy in copies:
        copy.start()
    return copies


def chip_order(chips):
    return list(range(0, chips, 2)) + list(range(1, chips, 2))[::-1]


def ring_perm(chips):
    order = chip_order(chips)
    pairs = []
    for place, chip in enumerate(order):
        pairs.append((chip * 2, order[(place + 1) % chips] * 2))
        pairs.append((chip * 2 + 1, order[(place - 1) % chips] * 2 + 1))
    return pairs


def core_perm(chips):
    return [(dev, dev ^ 1) for dev in range(2 * chips)]


def state_kernel(k_hbm, v_hbm, out_ref, k_ref, v_ref, sems):
    for copy in copies_of([k_hbm, v_hbm], [k_ref, v_ref], sems):
        copy.wait()
    for head in range(HEADS):
        cols = pl.ds(head * HEAD, HEAD)
        state = lax.dot_general(
            k_ref[:, cols], v_ref[:, cols], (((0,), (0,)), ((), ())), preferred_element_type=F32
        )
        out_ref[cols, :] = state.astype(BF16)


def inside_kernel(count, *refs):
    q_ref, k_ref, v_ref = refs[count + 1 : count + 4]
    out_ref, sems = refs[2 * count + 1], refs[-1]
    copies = copies_of(refs[:count], refs[count + 1 : 2 * count + 1], sems)
    for copy in copies[:3]:
        copy.wait()
    ntok = q_ref.shape[0]
    causal = lax.broadcasted_iota(jnp.int32, (ntok, ntok), 0) >= lax.broadcasted_iota(
        jnp.int32, (ntok, ntok), 1
    )
    for head in range(HEADS):
        cols = pl.ds(head * HEAD, HEAD)
        scores = lax.dot_general(
            q_ref[:, cols], k_ref[:, cols], (((1,), (1,)), ((), ())), preferred_element_type=F32
        )
        scores = jnp.where(causal, scores, 0.0).astype(BF16)
        out_ref[:, cols] = jnp.dot(scores, v_ref[:, cols], preferred_element_type=F32)
    for copy in copies[3:]:
        copy.wait()


def attend_inside(arrays, after):
    count = len(arrays)
    outs = [pltpu.VMEM(a.shape, a.dtype) for a in arrays]
    outs.append(pltpu.VMEM(arrays[0].shape, F32))
    return pl.pallas_call(
        functools.partial(inside_kernel, count),
        out_shape=outs,
        in_specs=[HBM] * count + [pl.BlockSpec(memory_space=pl.ANY)],
        out_specs=[VMEM] * (count + 1),
        scratch_shapes=[pltpu.SemaphoreType.DMA((count,))],
        compiler_params=pltpu.CompilerParams(vmem_limit_bytes=LIMIT),
    )(*[in_hbm(a) for a in arrays], after)


def prefix_kernel(pieces_ref, extra_ref, out_ref):
    devices, share, cols = pieces_ref.shape
    owners = extra_ref.shape[0]
    total = jnp.zeros((share, cols), F32)
    for dev in range(devices):
        rows = jnp.concatenate([total, extra_ref[dev % owners]])
        out_ref[dev] = rows.astype(BF16)
        total += pieces_ref[dev].astype(F32)


def scan_states(states, dense):
    rows, cols = states.shape
    ntok, owners = dense.shape
    devices = lax.axis_size(BOTH)
    share = rows // devices
    top = dense.astype(BF16).astype(F32)
    extra = jnp.concatenate([top, dense - top]).T.reshape(owners, 2 * ntok // cols, cols)
    used = extra.shape[1]
    extra = jnp.pad(extra, ((0, 0), (0, -used % 8), (0, 0)))
    pieces = states.reshape(devices, share, cols)
    pieces = lax.all_to_all(pieces, BOTH, split_axis=0, concat_axis=0, tiled=True)
    whole_tiles = share % 16 == 0
    if whole_tiles:
        out = jax.ShapeDtypeStruct((devices, share + extra.shape[1], cols), BF16)
        sums = call(prefix_kernel, out, [VMEM] * 2, 0, pieces, extra)
    else:
        earlier = jnp.arange(devices)[:, None] > jnp.arange(devices)[None, :]
        sums = jnp.dot(
            earlier.astype(BF16),
            pieces.reshape(devices, share * cols),
            preferred_element_type=F32,
        ).reshape(devices, share, cols)
        extra_all = jnp.concatenate([extra] * (devices // owners))
        sums = jnp.concatenate([sums, extra_all], axis=1).astype(BF16)
    sums = lax.all_to_all(sums, BOTH, split_axis=0, concat_axis=0, tiled=True)
    split = lax.dynamic_slice_in_dim(
        sums[:, share : share + used], lax.axis_index("seg") * owners, owners
    )
    split = split.reshape(owners, 2, ntok).astype(F32)
    mine = (split[:, 0] + split[:, 1]).T
    if not whole_tiles:
        sums = sums[:, :share].reshape(rows // HEAD, HEAD, cols)
        share = HEAD
    return sums, share, mine


def rms(rows, gain):
    mean_sq = jnp.mean(rows * rows, axis=1, keepdims=True)
    return rows * lax.rsqrt(mean_sq + 1e-06) * gain


def route_kernel(
    share, q_ref, sums_ref, inside_ref, hidden_ref, gain_ref, proj_ref, moe_gain_ref, *outs
):
    ntok, width = q_ref.shape
    slabs = HEAD // share
    attended = []
    for head in range(HEADS):
        cols = pl.ds(head * HEAD, HEAD)
        earlier = jnp.concatenate(
            [sums_ref[head * slabs + i, pl.ds(0, share), :] for i in range(slabs)]
        )
        carried = jnp.dot(q_ref[:, cols], earlier, preferred_element_type=F32)
        attended.append(carried + inside_ref[:, cols])
    attended = jnp.concatenate(attended, axis=1)
    normed = rms(attended, gain_ref[...]).astype(BF16)
    mixed = hidden_ref[...].astype(F32) + jnp.dot(
        normed, proj_ref[...], preferred_element_type=F32
    )
    outs[0][...] = mixed
    routed = rms(mixed, moe_gain_ref[...]).astype(BF16)
    cut = ntok // HALVES
    for half in range(HALVES):
        outs[1 + half][...] = routed[half * cut : (half + 1) * cut]


def expert_kernel(
    chips, step, first, pair, dense, w_gate, w_up, w_down, here_ref, there_ref, *outs
):
    copies = []
    if pair:
        outs[4][...] = outs[0][...].astype(F32) + outs[1][...].astype(F32)
        outs = outs[2:4]
    elif len(outs) > 2:
        staged = outs[2:5]
        copies = copies_of([w_gate, w_up, w_down], staged, outs[5])
        w_gate, w_up, w_down = staged
    me = lax.axis_index("ctx")
    core, chip = me % 2, me // 2
    place = jnp.where(chip % 2 == 0, chip // 2, chips - 1 - chip // 2)
    way = 1 - 2 * core

    def device_at(offset, plane):
        spot = (place + offset + chips) % chips
        return jnp.where(2 * spot < chips, 2 * spot, 2 * (chips - spot) - 1) * 2 + plane

    planes = [core] if step in (0, chips // 2) else [core, 1 - core]
    sources = [device_at(-way * step, plane) for plane in planes]
    sources += [device_at(way * step, 1 - plane) for plane in planes]
    rows = jnp.concatenate([here_ref[...], there_ref[...]])
    count = here_ref.shape[0]
    for copy in copies[:2]:
        copy.wait()
    gate = jnp.dot(rows, w_gate[0], preferred_element_type=F32)
    upper = jnp.dot(rows, w_up[0], preferred_element_type=F32)
    inner = (gate / (1.0 + jnp.exp(-gate)) * upper).astype(BF16)
    for copy in copies[2:]:
        copy.wait()
    result = jnp.dot(inner, w_down[0], preferred_element_type=F32)
    block = len(sources)
    cut = 2 * count // block
    table = dense[pl.ds(first, cut), :]
    lane = lax.broadcasted_iota(jnp.int32, table.shape, 1)
    scales = [
        jnp.sum(jnp.where(lane == source, table, 0.0), axis=1, keepdims=True) for source in sources
    ]
    result = (result * jnp.concatenate(scales)).astype(BF16)
    outs[0][...] = result[:count]
    outs[1][...] = result[count:]


def expert(here, there, chips, step, first, dense, weights, staging, pair):
    outs = [jax.ShapeDtypeStruct(here.shape, BF16)] * 2
    specs, scratch = [VMEM] * 3, []
    if staging:
        outs += [pltpu.VMEM(w.shape, w.dtype) for w in weights]
        specs, scratch = [HBM] * 3, [pltpu.SemaphoreType.DMA((3,))]
        weights = [in_hbm(w) for w in weights]
    if pair:
        outs.append(jax.ShapeDtypeStruct(pair[0].shape, F32))
    return pl.pallas_call(
        functools.partial(expert_kernel, chips, step, first, len(pair)),
        out_shape=outs,
        in_specs=[VMEM] + specs + [VMEM] * (2 + len(pair)),
        out_specs=[VMEM] * len(outs),
        scratch_shapes=scratch,
        compiler_params=pltpu.CompilerParams(vmem_limit_bytes=LIMIT),
        cost_estimate=pl.CostEstimate(
            flops=12 * here.size * weights[0].shape[2], bytes_accessed=0, transcendentals=0
        ),
    )(dense, *weights, here, there, *pair)


def body(
    hidden_in,
    queries,
    key_rows,
    values,
    norm_gain,
    out_proj,
    moe_gain,
    w_gate,
    w_up,
    w_down,
    expert_ids,
    route_scale,
):
    ntok, width = queries.shape
    owners = lax.axis_size("ctx")
    chips = owners // 2
    out = jax.ShapeDtypeStruct((HEADS * HEAD, HEAD), BF16)
    states = pl.pallas_call(
        state_kernel,
        out_shape=out,
        in_specs=[pl.BlockSpec(memory_space=pltpu.HBM)] * 2,
        out_specs=VMEM,
        scratch_shapes=[pltpu.VMEM((ntok, width), BF16)] * 2 + [pltpu.SemaphoreType.DMA((2,))],
        compiler_params=pltpu.CompilerParams(vmem_limit_bytes=LIMIT),
    )(in_hbm(key_rows), in_hbm(values))
    scales = route_scale.astype(F32)
    weight = scales / jnp.sum(scales, axis=1, keepdims=True)
    grid = jnp.arange(owners, dtype=jnp.int32)
    dense = jnp.sum(
        jnp.where(expert_ids[:, :, None] == grid[None, None, :], weight[:, :, None], 0.0), axis=1
    )
    sums, share, dense = scan_states(states, dense)

    out = jax.ShapeDtypeStruct((ntok, width), F32)
    arrays = [queries, key_rows, values, hidden_in, norm_gain[None, :], out_proj, moe_gain[None, :]]
    queries, _, _, hidden_in, norm_gain, out_proj, moe_gain, inside = attend_inside(arrays, states)
    cut = ntok // HALVES
    outs = [out] + [jax.ShapeDtypeStruct((cut, width), BF16)] * HALVES
    mixed, *routed = call(
        functools.partial(route_kernel, share),
        outs,
        [VMEM] * 7,
        2 * ntok * width * (HEAD + width),
        queries,
        sums,
        inside,
        hidden_in,
        norm_gain,
        out_proj,
        moe_gain,
    )

    far = chips // 2
    ring, swap = ring_perm(chips), core_perm(chips)

    def send(rows):
        return lax.ppermute(rows, "ctx", ring)

    def cross(rows):
        return lax.ppermute(rows, "ctx", swap)

    weights = [w_gate, w_up, w_down]
    kept, partner, here, there, summed, done = {}, {}, {}, {}, {}, {}

    def work(half, step):
        nonlocal weights
        pair = [] if step < 2 else [kept[half, step - 1], partner[half, step - 1]]
        arrived, kept[half, step], *more = expert(
            here[half, step],
            there[half, step],
            chips,
            step,
            half * cut,
            dense,
            weights,
            half == step == 0,
            pair,
        )
        if half == step == 0:
            weights = more
        if pair:
            summed[half, step - 1] = more[0]
        done[half, step] = kept[half, step]
        partner[half, step] = arrived if step == 0 else cross(arrived)

    for half in range(HALVES):
        here[half, 0], there[half, 0] = routed[half], cross(routed[half])
        chunk = jnp.concatenate([here[half, 0], there[half, 0]])
        here[half, 1] = send(chunk)
    for half in range(HALVES):
        work(half, 0)
    for step in range(1, far + 1):
        for half in range(HALVES):
            before = done[max(half, 2 - step), step - 1]
            chunk = lax.optimization_barrier((here[half, step], before))[0]
            there[half, step] = cross(chunk)
            if step < far:
                here[half, step + 1] = send(chunk if step + 1 < far else chunk[:cut])
            work(half, step)

    rows = []
    for half in range(HALVES):
        moving = None
        for step in range(far, 0, -1):
            if step < far:
                total = summed[half, step]
            else:
                total = kept[half, step].astype(F32) + partner[half, step].astype(F32)
            if moving is not None:
                if moving.shape[0] < total.shape[0]:
                    moving = jnp.concatenate([moving, jnp.zeros_like(moving)])
                total = total + moving.astype(F32)
            moving = send(total.astype(BF16))
        if moving.shape[0] < 2 * cut:
            moving = jnp.concatenate([moving, jnp.zeros_like(moving)])
        moving = moving.astype(F32)
        home = cross((moving[:cut] + kept[half, 0].astype(F32)).astype(BF16))
        rows.append(
            mixed[half * cut : (half + 1) * cut]
            + (moving[cut:] + partner[half, 0].astype(F32) + home.astype(F32))
        )
    return jnp.concatenate(rows).astype(BF16)


def solution(mesh):
    rows = P(BOTH, None)
    expert_spec = P("ctx", None, None)
    return jax.shard_map(
        body,
        mesh=mesh,
        in_specs=(rows,) * 4 + (P(),) * 3 + (expert_spec,) * 3 + (rows,) * 2,
        out_specs=rows,
        check_vma=False,
    )
```

```python
import functools

import jax
import jax.numpy as jnp
from jax import lax
from jax.experimental import pallas as pl
from jax.experimental.pallas import tpu as pltpu
from jax.sharding import PartitionSpec as P

HEADS = 8
HEAD = 128
HALVES = 2
BOTH = ("seg", "ctx")
F32 = jnp.float32
BF16 = jnp.bfloat16
VMEM = pl.BlockSpec(memory_space=pltpu.VMEM)
HBM = pl.BlockSpec(memory_space=pltpu.HBM)
LIMIT = 16 * 1024 * 1024


def call(kernel, out_shape, in_specs, flops, *operands):
    many = isinstance(out_shape, list)
    return pl.pallas_call(
        kernel,
        out_shape=out_shape,
        in_specs=in_specs,
        out_specs=[VMEM] * len(out_shape) if many else VMEM,
        compiler_params=pltpu.CompilerParams(vmem_limit_bytes=LIMIT),
        cost_estimate=pl.CostEstimate(flops=flops, bytes_accessed=0, transcendentals=0),
    )(*operands)


def in_hbm(array):
    return pltpu.with_memory_space_constraint(array, pltpu.HBM)


def copies_of(sources, targets, sems):
    copies = [
        pltpu.make_async_copy(source, target, sems.at[i])
        for i, (source, target) in enumerate(zip(sources, targets))
    ]
    for copy in copies:
        copy.start()
    return copies


def chip_order(chips):
    return list(range(0, chips, 2)) + list(range(1, chips, 2))[::-1]


def ring_perm(chips, shift):
    order = chip_order(chips)
    pairs = []
    for place, chip in enumerate(order):
        pairs.append((chip * 2, order[(place + shift) % chips] * 2))
        pairs.append((chip * 2 + 1, order[(place - shift) % chips] * 2 + 1))
    return pairs


def core_perm(chips):
    return [(dev, dev ^ 1) for dev in range(2 * chips)]


def state_kernel(k_hbm, v_hbm, out_ref, k_ref, v_ref, sems):
    for copy in copies_of([k_hbm, v_hbm], [k_ref, v_ref], sems):
        copy.wait()
    for head in range(HEADS):
        cols = pl.ds(head * HEAD, HEAD)
        state = lax.dot_general(
            k_ref[:, cols], v_ref[:, cols], (((0,), (0,)), ((), ())), preferred_element_type=F32
        )
        out_ref[cols, :] = state.astype(BF16)


def inside_kernel(count, *refs):
    q_ref, k_ref, v_ref = refs[count + 1 : count + 4]
    out_hbm, out_ref, sems = refs[2 * count + 1 :]
    copies = copies_of(refs[:count], refs[count + 1 : 2 * count + 1], sems)
    for copy in copies[:3]:
        copy.wait()
    ntok = q_ref.shape[0]
    causal = lax.broadcasted_iota(jnp.int32, (ntok, ntok), 0) >= lax.broadcasted_iota(
        jnp.int32, (ntok, ntok), 1
    )
    for head in range(HEADS):
        cols = pl.ds(head * HEAD, HEAD)
        scores = lax.dot_general(
            q_ref[:, cols], k_ref[:, cols], (((1,), (1,)), ((), ())), preferred_element_type=F32
        )
        scores = jnp.where(causal, scores, 0.0).astype(BF16)
        out_ref[:, cols] = jnp.dot(scores, v_ref[:, cols], preferred_element_type=F32)
    copy = pltpu.make_async_copy(out_ref, out_hbm, sems.at[count])
    copy.start()
    for copy in copies[3:] + [copy]:
        copy.wait()


def attend_inside(arrays, after):
    count = len(arrays)
    outs = [pltpu.VMEM(a.shape, a.dtype) for a in arrays]
    outs.append(pltpu.HBM(arrays[0].shape, F32))
    return pl.pallas_call(
        functools.partial(inside_kernel, count),
        out_shape=outs,
        in_specs=[HBM] * count + [pl.BlockSpec(memory_space=pl.ANY)],
        out_specs=[VMEM] * count + [HBM],
        scratch_shapes=[pltpu.VMEM(arrays[0].shape, F32), pltpu.SemaphoreType.DMA((count + 1,))],
        compiler_params=pltpu.CompilerParams(vmem_limit_bytes=LIMIT),
    )(*[in_hbm(a) for a in arrays], after)


def prefix_kernel(pieces_ref, extra_ref, out_ref):
    devices, share, cols = pieces_ref.shape
    owners = extra_ref.shape[0]
    total = jnp.zeros((share, cols), F32)
    for dev in range(devices):
        rows = jnp.concatenate([total, extra_ref[dev % owners]])
        out_ref[dev] = rows.astype(BF16)
        total += pieces_ref[dev].astype(F32)


def scan_states(states, dense):
    rows, cols = states.shape
    ntok, owners = dense.shape
    devices = lax.axis_size(BOTH)
    share = rows // devices
    top = dense.astype(BF16).astype(F32)
    split = jnp.stack([top.T, (dense - top).T], axis=1)
    pairs = split.reshape(owners // 2, 2, 2, ntok)
    split = jnp.concatenate([split, pairs[:, ::-1].reshape(split.shape)], axis=1)
    extra = split.reshape(owners, 4 * ntok // cols, cols)
    used = extra.shape[1]
    extra = jnp.pad(extra, ((0, 0), (0, -used % 8), (0, 0)))
    pieces = states.reshape(devices, share, cols)
    pieces = lax.all_to_all(pieces, BOTH, split_axis=0, concat_axis=0, tiled=True)
    whole_tiles = share % 16 == 0
    if whole_tiles:
        out = jax.ShapeDtypeStruct((devices, share + extra.shape[1], cols), BF16)
        sums = call(prefix_kernel, out, [VMEM] * 2, 0, pieces, extra)
    else:
        earlier = jnp.arange(devices)[:, None] > jnp.arange(devices)[None, :]
        sums = jnp.dot(
            earlier.astype(BF16),
            pieces.reshape(devices, share * cols),
            preferred_element_type=F32,
        ).reshape(devices, share, cols)
        extra_all = jnp.concatenate([extra] * (devices // owners))
        sums = jnp.concatenate([sums, extra_all], axis=1).astype(BF16)
    sums = lax.all_to_all(sums, BOTH, split_axis=0, concat_axis=0, tiled=True)
    split = lax.dynamic_slice_in_dim(
        sums[:, share : share + used], lax.axis_index("seg") * owners, owners
    )
    split = split.reshape(owners, 4, ntok).astype(F32)
    mine = jnp.concatenate([split[:, 0] + split[:, 1], split[:, 2] + split[:, 3]]).T
    if not whole_tiles:
        sums = sums[:, :share].reshape(rows // HEAD, HEAD, cols)
        share = HEAD
    return sums, share, mine


def rms(rows, gain):
    mean_sq = jnp.mean(rows * rows, axis=1, keepdims=True)
    return rows * lax.rsqrt(mean_sq + 1e-06) * gain


def route_kernel(
    share, sums_ref, q_ref, proj_ref, gain_ref, moe_gain_ref, inside_hbm, hidden_hbm, *refs
):
    outs, (inside_ref, hidden_ref, sems) = refs[: 1 + HALVES], refs[1 + HALVES :]
    copies = copies_of([inside_hbm, hidden_hbm], [inside_ref, hidden_ref], sems)
    ntok, width = q_ref.shape
    slabs = HEAD // share
    attended = []
    for head in range(HEADS):
        cols = pl.ds(head * HEAD, HEAD)
        earlier = jnp.concatenate(
            [sums_ref[head * slabs + i, pl.ds(0, share), :] for i in range(slabs)]
        )
        attended.append(jnp.dot(q_ref[:, cols], earlier, preferred_element_type=F32))
    for copy in copies:
        copy.wait()
    attended = jnp.concatenate(attended, axis=1) + inside_ref[...]
    normed = rms(attended, gain_ref[...]).astype(BF16)
    mixed = hidden_ref[...].astype(F32) + jnp.dot(
        normed, proj_ref[...], preferred_element_type=F32
    )
    outs[0][...] = mixed
    routed = rms(mixed, moe_gain_ref[...]).astype(BF16)
    cut = ntok // HALVES
    for half in range(HALVES):
        outs[1 + half][...] = routed[half * cut : (half + 1) * cut]


def expert_kernel(chips, step, first, dense, rows_ref, *refs):
    weights, out_ref, refs = refs[:6], refs[6], refs[7:]
    copies = []
    if refs:
        copies = copies_of(weights, refs[:6], refs[6])
        weights = refs[:6]
    me = lax.axis_index("ctx")
    core, chip = me % 2, me // 2
    place = jnp.where(chip % 2 == 0, chip // 2, chips - 1 - chip // 2)
    spot = (place - (1 - 2 * core) * step + chips) % chips
    chip = jnp.where(2 * spot < chips, 2 * spot, 2 * (chips - spot) - 1)
    planes = [core] if step in (0, chips // 2) else [core, 1 - core]
    count = rows_ref.shape[0]
    cut = count // len(planes)
    table = dense[pl.ds(first, cut), :]
    lane = lax.broadcasted_iota(jnp.int32, table.shape, 1)
    rows = rows_ref[...]
    total = jnp.zeros(rows.shape, F32)
    for which in range(2):
        w_gate, w_up, w_down = weights[3 * which : 3 * which + 3]
        for copy in copies[3 * which : 3 * which + 3]:
            copy.wait()
        gate = jnp.dot(rows, w_gate[0], preferred_element_type=F32)
        upper = jnp.dot(rows, w_up[0], preferred_element_type=F32)
        inner = (gate / (1.0 + jnp.exp(-gate)) * upper).astype(BF16)
        result = jnp.dot(inner, w_down[0], preferred_element_type=F32)
        scales = []
        for plane in planes:
            column = which * 2 * chips + chip * 2 + plane
            picked = jnp.where(lane == column, table, 0.0)
            scales.append(jnp.sum(picked, axis=1, keepdims=True))
        total += result * jnp.concatenate(scales)
    out_ref[...] = total


def expert(rows, chips, step, first, dense, weights, staging):
    outs, specs, scratch = [jax.ShapeDtypeStruct(rows.shape, F32)], [VMEM] * 6, []
    if staging:
        outs += [pltpu.VMEM(w.shape, w.dtype) for w in weights]
        specs, scratch = [HBM] * 6, [pltpu.SemaphoreType.DMA((6,))]
        weights = [in_hbm(w) for w in weights]
    return pl.pallas_call(
        functools.partial(expert_kernel, chips, step, first),
        out_shape=outs,
        in_specs=[VMEM] * 2 + specs,
        out_specs=[VMEM] * len(outs),
        scratch_shapes=scratch,
        compiler_params=pltpu.CompilerParams(vmem_limit_bytes=LIMIT),
        cost_estimate=pl.CostEstimate(
            flops=0, bytes_accessed=0, transcendentals=0
        ),
    )(dense, rows, *weights)


def body(
    hidden_in,
    queries,
    key_rows,
    values,
    norm_gain,
    out_proj,
    moe_gain,
    w_gate,
    w_up,
    w_down,
    expert_ids,
    route_scale,
):
    ntok, width = queries.shape
    owners = lax.axis_size("ctx")
    chips = owners // 2
    out = jax.ShapeDtypeStruct((HEADS * HEAD, HEAD), BF16)
    states = pl.pallas_call(
        state_kernel,
        out_shape=out,
        in_specs=[pl.BlockSpec(memory_space=pltpu.HBM)] * 2,
        out_specs=VMEM,
        scratch_shapes=[pltpu.VMEM((ntok, width), BF16)] * 2 + [pltpu.SemaphoreType.DMA((2,))],
        compiler_params=pltpu.CompilerParams(vmem_limit_bytes=LIMIT),
    )(in_hbm(key_rows), in_hbm(values))
    scales = route_scale.astype(F32)
    weight = scales / jnp.sum(scales, axis=1, keepdims=True)
    grid = jnp.arange(owners, dtype=jnp.int32)
    dense = jnp.sum(
        jnp.where(expert_ids[:, :, None] == grid[None, None, :], weight[:, :, None], 0.0), axis=1
    )
    sums, share, dense = scan_states(states, dense)

    out = jax.ShapeDtypeStruct((ntok, width), F32)
    arrays = [queries, key_rows, values, out_proj, norm_gain[None, :], moe_gain[None, :]]
    queries, _, _, out_proj, norm_gain, moe_gain, inside = attend_inside(arrays, states)
    cut = ntok // HALVES
    held = [inside, hidden_in]
    mixed, *routed = pl.pallas_call(
        functools.partial(route_kernel, share),
        out_shape=[out] + [jax.ShapeDtypeStruct((cut, width), BF16)] * HALVES,
        in_specs=[VMEM] * 5 + [HBM] * len(held),
        out_specs=[VMEM] * (1 + HALVES),
        scratch_shapes=[pltpu.VMEM(a.shape, a.dtype) for a in held]
        + [pltpu.SemaphoreType.DMA((len(held),))],
        compiler_params=pltpu.CompilerParams(vmem_limit_bytes=LIMIT),
    )(sums, queries, out_proj, norm_gain, moe_gain, *[in_hbm(a) for a in held])

    far = chips // 2
    ring, back, swap = ring_perm(chips, 1), ring_perm(chips, -1), core_perm(chips)

    def hold(rows, *before):
        return lax.optimization_barrier((rows, before))[0]

    def send(rows, way):
        return lax.ppermute(rows, "ctx", way)

    def cross(rows):
        return lax.ppermute(rows, "ctx", swap)

    weights = [w_gate, w_up, w_down]
    weights += [cross(w) for w in weights]
    here, done = {}, {}
    first = []
    for half in range(HALVES):
        own, other = hold([routed[half], cross(routed[half])], *first)
        here[half, 0] = jnp.concatenate([own, other])
        first = [here[half, 0]]
        here[half, 1] = send(here[half, 0], ring)
    at_home, *weights = expert(jnp.concatenate(routed), chips, 0, 0, dense, weights, True)

    def work(half, step, *before):
        rows = hold(here[half, step], *before)
        done[half, step] = expert(rows, chips, step, half * cut, dense, weights, False)[0]

    for step in range(1, far):
        for half in range(HALVES):
            ready = at_home if step == 1 else done[half, step - 1]
            chunk = hold(here[half, step], ready)
            here[half, step + 1] = send(chunk if step + 1 < far else chunk[:cut], ring)
            if step + 1 < far:
                work(half, step)
    before = []
    for half in range(HALVES):
        for step in (far - 1, far):
            work(half, step, *before)
            before = [done[half, step]]

    moving = [send(done[half, far].astype(BF16), back).astype(F32) for half in range(HALVES)]
    if far > 1:
        moving = [jnp.concatenate([part, jnp.zeros_like(part)]) for part in moving]
    for step in range(far - 1, 0, -1):
        passed = []
        for half in range(HALVES):
            total = (done[half, step] + hold(moving[half], *passed)).astype(BF16)
            passed = [moving[half]]
            moving[half] = send(total, back).astype(F32)
    rows = []
    for half in range(HALVES):
        home = moving[half][:cut]
        if far > 1:
            home = home + cross(moving[half][cut:].astype(BF16)).astype(F32)
        here_rows = slice(half * cut, (half + 1) * cut)
        rows.append(mixed[here_rows] + (at_home[here_rows] + home))
    return jnp.concatenate(rows).astype(BF16)


def solution(mesh):
    rows = P(BOTH, None)
    expert_spec = P("ctx", None, None)
    return jax.shard_map(
        body,
        mesh=mesh,
        in_specs=(rows,) * 4 + (P(),) * 3 + (expert_spec,) * 3 + (rows,) * 2,
        out_specs=rows,
        check_vma=False,
    )
```

```python
import functools

import jax
import jax.numpy as jnp
from jax import lax
from jax.experimental import pallas as pl
from jax.experimental.pallas import tpu as pltpu
from jax.sharding import PartitionSpec as P

HEADS = 8
HEAD = 128
BOTH = ("seg", "ctx")
F32 = jnp.float32
BF16 = jnp.bfloat16
VMEM = pl.BlockSpec(memory_space=pltpu.VMEM)
HBM = pl.BlockSpec(memory_space=pltpu.HBM)
LIMIT = 16 * 1024 * 1024


def call(kernel, out_shape, in_specs, flops, *operands):
    many = isinstance(out_shape, list)
    return pl.pallas_call(
        kernel,
        out_shape=out_shape,
        in_specs=in_specs,
        out_specs=[VMEM] * len(out_shape) if many else VMEM,
        compiler_params=pltpu.CompilerParams(vmem_limit_bytes=LIMIT),
        cost_estimate=pl.CostEstimate(flops=flops, bytes_accessed=0, transcendentals=0),
    )(*operands)


def in_hbm(array):
    return pltpu.with_memory_space_constraint(array, pltpu.HBM)


def copies_of(sources, targets, sems):
    copies = [
        pltpu.make_async_copy(source, target, sems.at[i])
        for i, (source, target) in enumerate(zip(sources, targets))
    ]
    for copy in copies:
        copy.start()
    return copies


def chip_order(chips):
    return list(range(0, chips, 2)) + list(range(1, chips, 2))[::-1]


def ring_perm(chips, shift):
    order = chip_order(chips)
    pairs = []
    for place, chip in enumerate(order):
        pairs.append((chip * 2, order[(place + shift) % chips] * 2))
        pairs.append((chip * 2 + 1, order[(place - shift) % chips] * 2 + 1))
    return pairs


def core_perm(chips):
    return [(dev, dev ^ 1) for dev in range(2 * chips)]


def state_kernel(k_hbm, v_hbm, out_ref, k_ref, v_ref, sems):
    for copy in copies_of([k_hbm, v_hbm], [k_ref, v_ref], sems):
        copy.wait()
    for head in range(HEADS):
        cols = pl.ds(head * HEAD, HEAD)
        state = lax.dot_general(
            k_ref[:, cols], v_ref[:, cols], (((0,), (0,)), ((), ())), preferred_element_type=F32
        )
        out_ref[cols, :] = state.astype(BF16)


def inside_kernel(count, *refs):
    q_ref, k_ref, v_ref = refs[count + 1 : count + 4]
    out_hbm, out_ref, sems = refs[2 * count + 1 :]
    copies = copies_of(refs[:count], refs[count + 1 : 2 * count + 1], sems)
    for copy in copies[:3]:
        copy.wait()
    ntok = q_ref.shape[0]
    causal = lax.broadcasted_iota(jnp.int32, (ntok, ntok), 0) >= lax.broadcasted_iota(
        jnp.int32, (ntok, ntok), 1
    )
    for head in range(HEADS):
        cols = pl.ds(head * HEAD, HEAD)
        scores = lax.dot_general(
            q_ref[:, cols], k_ref[:, cols], (((1,), (1,)), ((), ())), preferred_element_type=F32
        )
        scores = jnp.where(causal, scores, 0.0).astype(BF16)
        out_ref[:, cols] = jnp.dot(scores, v_ref[:, cols], preferred_element_type=F32)
    copy = pltpu.make_async_copy(out_ref, out_hbm, sems.at[count])
    copy.start()
    for copy in copies[3:] + [copy]:
        copy.wait()


def attend_inside(arrays, after):
    count = len(arrays)
    outs = [pltpu.VMEM(a.shape, a.dtype) for a in arrays]
    outs.append(pltpu.HBM(arrays[0].shape, F32))
    return pl.pallas_call(
        functools.partial(inside_kernel, count),
        out_shape=outs,
        in_specs=[HBM] * count + [pl.BlockSpec(memory_space=pl.ANY)],
        out_specs=[VMEM] * count + [HBM],
        scratch_shapes=[pltpu.VMEM(arrays[0].shape, F32), pltpu.SemaphoreType.DMA((count + 1,))],
        compiler_params=pltpu.CompilerParams(vmem_limit_bytes=LIMIT),
    )(*[in_hbm(a) for a in arrays], after)


def prefix_kernel(pieces_ref, extra_ref, out_ref):
    devices, share, cols = pieces_ref.shape
    owners = extra_ref.shape[0]
    total = jnp.zeros((share, cols), F32)
    for dev in range(devices):
        rows = jnp.concatenate([total, extra_ref[dev % owners]])
        out_ref[dev] = rows.astype(BF16)
        total += pieces_ref[dev].astype(F32)


def scan_states(states, dense):
    rows, cols = states.shape
    ntok, owners = dense.shape
    devices = lax.axis_size(BOTH)
    share = rows // devices
    top = dense.astype(BF16).astype(F32)
    split = jnp.stack([top.T, (dense - top).T], axis=1)
    pairs = split.reshape(owners // 2, 2, 2, ntok)
    split = jnp.concatenate([split, pairs[:, ::-1].reshape(split.shape)], axis=1)
    extra = split.reshape(owners, 4 * ntok // cols, cols)
    used = extra.shape[1]
    extra = jnp.pad(extra, ((0, 0), (0, -used % 8), (0, 0)))
    pieces = states.reshape(devices, share, cols)
    pieces = lax.all_to_all(pieces, BOTH, split_axis=0, concat_axis=0, tiled=True)
    whole_tiles = share % 16 == 0
    if whole_tiles:
        out = jax.ShapeDtypeStruct((devices, share + extra.shape[1], cols), BF16)
        sums = call(prefix_kernel, out, [VMEM] * 2, 0, pieces, extra)
    else:
        earlier = jnp.arange(devices)[:, None] > jnp.arange(devices)[None, :]
        sums = jnp.dot(
            earlier.astype(BF16),
            pieces.reshape(devices, share * cols),
            preferred_element_type=F32,
        ).reshape(devices, share, cols)
        extra_all = jnp.concatenate([extra] * (devices // owners))
        sums = jnp.concatenate([sums, extra_all], axis=1).astype(BF16)
    sums = lax.all_to_all(sums, BOTH, split_axis=0, concat_axis=0, tiled=True)
    split = lax.dynamic_slice_in_dim(
        sums[:, share : share + used], lax.axis_index("seg") * owners, owners
    )
    split = split.reshape(owners, 4, ntok).astype(F32)
    mine = jnp.concatenate([split[:, 0] + split[:, 1], split[:, 2] + split[:, 3]]).T
    if not whole_tiles:
        sums = sums[:, :share].reshape(rows // HEAD, HEAD, cols)
        share = HEAD
    return sums, share, mine


def rms(rows, gain):
    mean_sq = jnp.mean(rows * rows, axis=1, keepdims=True)
    return rows * lax.rsqrt(mean_sq + 1e-06) * gain


def route_kernel(
    share, sums_ref, q_ref, proj_ref, gain_ref, moe_gain_ref, inside_hbm, hidden_hbm, *refs
):
    mixed_ref, routed_ref, inside_ref, hidden_ref, sems = refs
    copies = copies_of([inside_hbm, hidden_hbm], [inside_ref, hidden_ref], sems)
    ntok, width = q_ref.shape
    slabs = HEAD // share
    attended = []
    for head in range(HEADS):
        cols = pl.ds(head * HEAD, HEAD)
        earlier = jnp.concatenate(
            [sums_ref[head * slabs + i, pl.ds(0, share), :] for i in range(slabs)]
        )
        attended.append(jnp.dot(q_ref[:, cols], earlier, preferred_element_type=F32))
    for copy in copies:
        copy.wait()
    attended = jnp.concatenate(attended, axis=1) + inside_ref[...]
    normed = rms(attended, gain_ref[...]).astype(BF16)
    mixed = hidden_ref[...].astype(F32) + jnp.dot(
        normed, proj_ref[...], preferred_element_type=F32
    )
    mixed_ref[...] = mixed
    routed_ref[...] = rms(mixed, moe_gain_ref[...]).astype(BF16)


def expert_kernel(chips, offset, flip, dense, rows_ref, *refs):
    weights, out_ref, refs = refs[:6], refs[6], refs[7:]
    copies = []
    if refs:
        copies = copies_of(weights, refs[:6], refs[6])
        weights = refs[:6]
    me = lax.axis_index("ctx")
    core, chip = me % 2, me // 2
    place = jnp.where(chip % 2 == 0, chip // 2, chips - 1 - chip // 2)
    spot = (place - (1 - 2 * core) * offset + chips) % chips
    chip = jnp.where(2 * spot < chips, 2 * spot, 2 * (chips - spot) - 1)
    source = chip * 2 + (1 - core if flip else core)
    rows = rows_ref[...]
    table = dense[...]
    lane = lax.broadcasted_iota(jnp.int32, table.shape, 1)
    total = jnp.zeros(rows.shape, F32)
    for which in range(2):
        w_gate, w_up, w_down = weights[3 * which : 3 * which + 3]
        for copy in copies[3 * which : 3 * which + 3]:
            copy.wait()
        gate = jnp.dot(rows, w_gate[0], preferred_element_type=F32)
        upper = jnp.dot(rows, w_up[0], preferred_element_type=F32)
        inner = (gate / (1.0 + jnp.exp(-gate)) * upper).astype(BF16)
        result = jnp.dot(inner, w_down[0], preferred_element_type=F32)
        picked = jnp.where(lane == which * 2 * chips + source, table, 0.0)
        total += result * jnp.sum(picked, axis=1, keepdims=True)
    out_ref[...] = total


def expert(rows, chips, offset, flip, dense, weights, staging=False):
    outs, specs, scratch = [jax.ShapeDtypeStruct(rows.shape, F32)], [VMEM] * 6, []
    if staging:
        outs += [pltpu.VMEM(w.shape, w.dtype) for w in weights]
        specs, scratch = [HBM] * 6, [pltpu.SemaphoreType.DMA((6,))]
        weights = [in_hbm(w) for w in weights]
    return pl.pallas_call(
        functools.partial(expert_kernel, chips, offset, flip),
        out_shape=outs,
        in_specs=[VMEM] * 2 + specs,
        out_specs=[VMEM] * len(outs),
        scratch_shapes=scratch,
        compiler_params=pltpu.CompilerParams(vmem_limit_bytes=LIMIT),
        cost_estimate=pl.CostEstimate(flops=0, bytes_accessed=0, transcendentals=0),
    )(dense, rows, *weights)


def body(
    hidden_in,
    queries,
    key_rows,
    values,
    norm_gain,
    out_proj,
    moe_gain,
    w_gate,
    w_up,
    w_down,
    expert_ids,
    route_scale,
):
    ntok, width = queries.shape
    owners = lax.axis_size("ctx")
    chips = owners // 2
    out = jax.ShapeDtypeStruct((HEADS * HEAD, HEAD), BF16)
    states = pl.pallas_call(
        state_kernel,
        out_shape=out,
        in_specs=[pl.BlockSpec(memory_space=pltpu.HBM)] * 2,
        out_specs=VMEM,
        scratch_shapes=[pltpu.VMEM((ntok, width), BF16)] * 2 + [pltpu.SemaphoreType.DMA((2,))],
        compiler_params=pltpu.CompilerParams(vmem_limit_bytes=LIMIT),
    )(in_hbm(key_rows), in_hbm(values))
    scales = route_scale.astype(F32)
    weight = scales / jnp.sum(scales, axis=1, keepdims=True)
    grid = jnp.arange(owners, dtype=jnp.int32)
    dense = jnp.sum(
        jnp.where(expert_ids[:, :, None] == grid[None, None, :], weight[:, :, None], 0.0), axis=1
    )
    sums, share, dense = scan_states(states, dense)

    out = jax.ShapeDtypeStruct((ntok, width), F32)
    arrays = [queries, key_rows, values, out_proj, norm_gain[None, :], moe_gain[None, :]]
    queries, _, _, out_proj, norm_gain, moe_gain, inside = attend_inside(arrays, states)
    held = [inside, hidden_in]
    mixed, routed = pl.pallas_call(
        functools.partial(route_kernel, share),
        out_shape=[out, jax.ShapeDtypeStruct((ntok, width), BF16)],
        in_specs=[VMEM] * 5 + [HBM] * len(held),
        out_specs=[VMEM] * 2,
        scratch_shapes=[pltpu.VMEM(a.shape, a.dtype) for a in held]
        + [pltpu.SemaphoreType.DMA((len(held),))],
        compiler_params=pltpu.CompilerParams(vmem_limit_bytes=LIMIT),
    )(sums, queries, out_proj, norm_gain, moe_gain, *[in_hbm(a) for a in held])

    far = chips // 2
    ring, back, swap = ring_perm(chips, 1), ring_perm(chips, -1), core_perm(chips)

    def hold(rows, *before):
        return lax.optimization_barrier((rows, before))[0]

    def send(rows, way):
        return lax.ppermute(rows, "ctx", way)

    weights = [w_gate, w_up, w_down]
    weights += [send(w, swap) for w in weights]
    here = [send(routed, ring), send(send(routed, swap), ring)]
    at_home, *weights = expert(routed, chips, 0, 0, dense, weights, True)
    done, ready = {}, [at_home, at_home]
    for step in range(1, far):
        passed = []
        for chain in range(2):
            rows = hold(here[chain], ready[chain], *passed)
            passed = [rows]
            if step + 1 < far or chain == 0:
                here[chain] = send(rows, ring)
            if step + 1 < far or chain:
                (done[chain, step],) = expert(rows, chips, step, chain, dense, weights)
                ready[chain] = done[chain, step]
            else:
                late = rows
    (done[0, far],) = expert(hold(here[0], *ready), chips, far, 0, dense, weights)
    if far > 1:
        late = hold(late, done[0, far])
        (done[0, far - 1],) = expert(late, chips, far - 1, 0, dense, weights)

    moving = [None, None]
    for step in range(far, 0, -1):
        for chain in range(2):
            if (chain, step) in done:
                total = done[chain, step]
                if moving[chain] is not None:
                    total = total + moving[chain]
                moving[chain] = send(total.astype(BF16), back).astype(F32)
    home = mixed + at_home
    if far > 1:
        home = home + send(moving[1].astype(BF16), swap).astype(F32)
    return (home + moving[0]).astype(BF16)


def solution(mesh):
    rows = P(BOTH, None)
    expert_spec = P("ctx", None, None)
    return jax.shard_map(
        body,
        mesh=mesh,
        in_specs=(rows,) * 4 + (P(),) * 3 + (expert_spec,) * 3 + (rows,) * 2,
        out_specs=rows,
        check_vma=False,
    )
```

```python
import functools

import jax
import jax.numpy as jnp
from jax import lax
from jax.experimental import pallas as pl
from jax.experimental.pallas import tpu as pltpu
from jax.sharding import PartitionSpec as P

HEADS = 8
HEAD = 128
BOTH = ("seg", "ctx")
F32 = jnp.float32
BF16 = jnp.bfloat16
VMEM = pl.BlockSpec(memory_space=pltpu.VMEM)
HBM = pl.BlockSpec(memory_space=pltpu.HBM)
LIMIT = 16 * 1024 * 1024


def call(kernel, out_shape, in_specs, flops, *operands):
    many = isinstance(out_shape, list)
    return pl.pallas_call(
        kernel,
        out_shape=out_shape,
        in_specs=in_specs,
        out_specs=[VMEM] * len(out_shape) if many else VMEM,
        compiler_params=pltpu.CompilerParams(vmem_limit_bytes=LIMIT),
        cost_estimate=pl.CostEstimate(flops=flops, bytes_accessed=0, transcendentals=0),
    )(*operands)


def in_hbm(array):
    return pltpu.with_memory_space_constraint(array, pltpu.HBM)


def copies_of(sources, targets, sems):
    copies = [
        pltpu.make_async_copy(source, target, sems.at[i])
        for i, (source, target) in enumerate(zip(sources, targets))
    ]
    for copy in copies:
        copy.start()
    return copies


def chip_order(chips):
    return list(range(0, chips, 2)) + list(range(1, chips, 2))[::-1]


def ring_perm(chips, shift):
    order = chip_order(chips)
    pairs = []
    for place, chip in enumerate(order):
        pairs.append((chip * 2, order[(place + shift) % chips] * 2))
        pairs.append((chip * 2 + 1, order[(place - shift) % chips] * 2 + 1))
    return pairs


def core_perm(chips):
    return [(dev, dev ^ 1) for dev in range(2 * chips)]


def state_kernel(k_hbm, v_hbm, out_ref, k_ref, v_ref, sems):
    for copy in copies_of([k_hbm, v_hbm], [k_ref, v_ref], sems):
        copy.wait()
    for head in range(HEADS):
        cols = pl.ds(head * HEAD, HEAD)
        state = lax.dot_general(
            k_ref[:, cols], v_ref[:, cols], (((0,), (0,)), ((), ())), preferred_element_type=F32
        )
        out_ref[cols, :] = state.astype(BF16)


def inside_kernel(count, *refs):
    q_ref, k_ref, v_ref = refs[count + 1 : count + 4]
    out_hbm, out_ref, sems = refs[2 * count + 1 :]
    copies = copies_of(refs[:count], refs[count + 1 : 2 * count + 1], sems)
    for copy in copies[:3]:
        copy.wait()
    ntok = q_ref.shape[0]
    causal = lax.broadcasted_iota(jnp.int32, (ntok, ntok), 0) >= lax.broadcasted_iota(
        jnp.int32, (ntok, ntok), 1
    )
    for head in range(HEADS):
        cols = pl.ds(head * HEAD, HEAD)
        scores = lax.dot_general(
            q_ref[:, cols], k_ref[:, cols], (((1,), (1,)), ((), ())), preferred_element_type=F32
        )
        scores = jnp.where(causal, scores, 0.0).astype(BF16)
        out_ref[:, cols] = jnp.dot(scores, v_ref[:, cols], preferred_element_type=F32)
    copy = pltpu.make_async_copy(out_ref, out_hbm, sems.at[count])
    copy.start()
    for copy in copies[3:] + [copy]:
        copy.wait()


def attend_inside(arrays, after):
    count = len(arrays)
    outs = [pltpu.VMEM(a.shape, a.dtype) for a in arrays]
    outs.append(pltpu.HBM(arrays[0].shape, F32))
    return pl.pallas_call(
        functools.partial(inside_kernel, count),
        out_shape=outs,
        in_specs=[HBM] * count + [pl.BlockSpec(memory_space=pl.ANY)],
        out_specs=[VMEM] * count + [HBM],
        scratch_shapes=[pltpu.VMEM(arrays[0].shape, F32), pltpu.SemaphoreType.DMA((count + 1,))],
        compiler_params=pltpu.CompilerParams(vmem_limit_bytes=LIMIT),
    )(*[in_hbm(a) for a in arrays], after)


def prefix_kernel(pieces_ref, extra_ref, out_ref):
    devices, share, cols = pieces_ref.shape
    owners = extra_ref.shape[0]
    total = jnp.zeros((share, cols), F32)
    for dev in range(devices):
        rows = jnp.concatenate([total, extra_ref[dev % owners]])
        out_ref[dev] = rows.astype(BF16)
        total += pieces_ref[dev].astype(F32)


def scan_states(states, dense):
    rows, cols = states.shape
    ntok, owners = dense.shape
    devices = lax.axis_size(BOTH)
    share = rows // devices
    top = dense.astype(BF16).astype(F32)
    split = jnp.stack([top.T, (dense - top).T], axis=1)
    pairs = split.reshape(owners // 2, 2, 2, ntok)
    split = jnp.concatenate([split, pairs[:, ::-1].reshape(split.shape)], axis=1)
    extra = split.reshape(owners, 4 * ntok // cols, cols)
    used = extra.shape[1]
    extra = jnp.pad(extra, ((0, 0), (0, -used % 8), (0, 0)))
    pieces = states.reshape(devices, share, cols)
    pieces = lax.all_to_all(pieces, BOTH, split_axis=0, concat_axis=0, tiled=True)
    whole_tiles = share % 16 == 0
    if whole_tiles:
        out = jax.ShapeDtypeStruct((devices, share + extra.shape[1], cols), BF16)
        sums = call(prefix_kernel, out, [VMEM] * 2, 0, pieces, extra)
    else:
        earlier = jnp.arange(devices)[:, None] > jnp.arange(devices)[None, :]
        sums = jnp.dot(
            earlier.astype(BF16),
            pieces.reshape(devices, share * cols),
            preferred_element_type=F32,
        ).reshape(devices, share, cols)
        extra_all = jnp.concatenate([extra] * (devices // owners))
        sums = jnp.concatenate([sums, extra_all], axis=1).astype(BF16)
    sums = lax.all_to_all(sums, BOTH, split_axis=0, concat_axis=0, tiled=True)
    split = lax.dynamic_slice_in_dim(
        sums[:, share : share + used], lax.axis_index("seg") * owners, owners
    )
    split = split.reshape(owners, 4, ntok).astype(F32)
    mine = jnp.concatenate([split[:, 0] + split[:, 1], split[:, 2] + split[:, 3]]).T
    if not whole_tiles:
        sums = sums[:, :share].reshape(rows // HEAD, HEAD, cols)
        share = HEAD
    return sums, share, mine


def rms(rows, gain):
    mean_sq = jnp.mean(rows * rows, axis=1, keepdims=True)
    return rows * lax.rsqrt(mean_sq + 1e-06) * gain


def route_kernel(
    share, sums_ref, q_ref, proj_ref, gain_ref, moe_gain_ref, inside_hbm, hidden_hbm, *refs
):
    mixed_ref, routed_ref, inside_ref, hidden_ref, sems = refs
    copies = copies_of([inside_hbm, hidden_hbm], [inside_ref, hidden_ref], sems)
    ntok, width = q_ref.shape
    slabs = HEAD // share
    attended = []
    for head in range(HEADS):
        cols = pl.ds(head * HEAD, HEAD)
        earlier = jnp.concatenate(
            [sums_ref[head * slabs + i, pl.ds(0, share), :] for i in range(slabs)]
        )
        attended.append(jnp.dot(q_ref[:, cols], earlier, preferred_element_type=F32))
    for copy in copies:
        copy.wait()
    attended = jnp.concatenate(attended, axis=1) + inside_ref[...]
    normed = rms(attended, gain_ref[...]).astype(BF16)
    mixed = hidden_ref[...].astype(F32) + jnp.dot(
        normed, proj_ref[...], preferred_element_type=F32
    )
    mixed_ref[...] = mixed
    routed_ref[...] = rms(mixed, moe_gain_ref[...]).astype(BF16)


def expert_kernel(chips, offset, flip, experts, dense, rows_ref, *refs):
    count = 3 * len(experts) if len(refs) < 13 else 6
    weights, out_ref, refs = refs[:count], refs[count], refs[count + 1 :]
    copies = []
    if refs:
        copies = copies_of(weights, refs[:6], refs[6])
        weights = refs[:6]
    me = lax.axis_index("ctx")
    core, chip = me % 2, me // 2
    place = jnp.where(chip % 2 == 0, chip // 2, chips - 1 - chip // 2)
    spot = (place - (1 - 2 * core) * offset + chips) % chips
    chip = jnp.where(2 * spot < chips, 2 * spot, 2 * (chips - spot) - 1)
    source = chip * 2 + (1 - core if flip else core)
    rows = rows_ref[...]
    table = dense[...]
    lane = lax.broadcasted_iota(jnp.int32, table.shape, 1)
    total = jnp.zeros(rows.shape, F32)
    for i, which in enumerate(experts):
        w_gate, w_up, w_down = weights[3 * i : 3 * i + 3]
        for copy in copies[3 * i : 3 * i + 3]:
            copy.wait()
        gate = jnp.dot(rows, w_gate[0], preferred_element_type=F32)
        upper = jnp.dot(rows, w_up[0], preferred_element_type=F32)
        inner = (gate / (1.0 + jnp.exp(-gate)) * upper).astype(BF16)
        result = jnp.dot(inner, w_down[0], preferred_element_type=F32)
        picked = jnp.where(lane == which * 2 * chips + source, table, 0.0)
        total += result * jnp.sum(picked, axis=1, keepdims=True)
    out_ref[...] = total
    for copy in copies[3 * len(experts) :]:
        copy.wait()


def expert(rows, chips, offset, flip, dense, weights, experts=(0, 1), staging=False):
    outs = [jax.ShapeDtypeStruct(rows.shape, F32)]
    specs, scratch = [VMEM] * len(weights), []
    if staging:
        outs += [pltpu.VMEM(w.shape, w.dtype) for w in weights]
        specs, scratch = [HBM] * 6, [pltpu.SemaphoreType.DMA((6,))]
        weights = [in_hbm(w) for w in weights]
    return pl.pallas_call(
        functools.partial(expert_kernel, chips, offset, flip, experts),
        out_shape=outs,
        in_specs=[VMEM] * 2 + specs,
        out_specs=[VMEM] * len(outs),
        scratch_shapes=scratch,
        compiler_params=pltpu.CompilerParams(vmem_limit_bytes=LIMIT),
        cost_estimate=pl.CostEstimate(flops=0, bytes_accessed=0, transcendentals=0),
    )(dense, rows, *weights)


def body(
    hidden_in,
    queries,
    key_rows,
    values,
    norm_gain,
    out_proj,
    moe_gain,
    w_gate,
    w_up,
    w_down,
    expert_ids,
    route_scale,
):
    ntok, width = queries.shape
    owners = lax.axis_size("ctx")
    chips = owners // 2
    out = jax.ShapeDtypeStruct((HEADS * HEAD, HEAD), BF16)
    states = pl.pallas_call(
        state_kernel,
        out_shape=out,
        in_specs=[pl.BlockSpec(memory_space=pltpu.HBM)] * 2,
        out_specs=VMEM,
        scratch_shapes=[pltpu.VMEM((ntok, width), BF16)] * 2 + [pltpu.SemaphoreType.DMA((2,))],
        compiler_params=pltpu.CompilerParams(vmem_limit_bytes=LIMIT),
    )(in_hbm(key_rows), in_hbm(values))
    scales = route_scale.astype(F32)
    weight = scales / jnp.sum(scales, axis=1, keepdims=True)
    grid = jnp.arange(owners, dtype=jnp.int32)
    dense = jnp.sum(
        jnp.where(expert_ids[:, :, None] == grid[None, None, :], weight[:, :, None], 0.0), axis=1
    )
    sums, share, dense = scan_states(states, dense)

    out = jax.ShapeDtypeStruct((ntok, width), F32)
    arrays = [queries, key_rows, values, out_proj, norm_gain[None, :], moe_gain[None, :]]
    queries, _, _, out_proj, norm_gain, moe_gain, inside = attend_inside(arrays, states)
    held = [inside, hidden_in]
    mixed, routed = pl.pallas_call(
        functools.partial(route_kernel, share),
        out_shape=[out, jax.ShapeDtypeStruct((ntok, width), BF16)],
        in_specs=[VMEM] * 5 + [HBM] * len(held),
        out_specs=[VMEM] * 2,
        scratch_shapes=[pltpu.VMEM(a.shape, a.dtype) for a in held]
        + [pltpu.SemaphoreType.DMA((len(held),))],
        compiler_params=pltpu.CompilerParams(vmem_limit_bytes=LIMIT),
    )(sums, queries, out_proj, norm_gain, moe_gain, *[in_hbm(a) for a in held])

    far = chips // 2
    ring, back, swap = ring_perm(chips, 1), ring_perm(chips, -1), core_perm(chips)

    def hold(rows, *before):
        return lax.optimization_barrier((rows, before))[0]

    def send(rows, way):
        return lax.ppermute(rows, "ctx", way)

    weights = [w_gate, w_up, w_down]
    weights += [send(w, swap) for w in weights]
    here = [send(routed, ring), send(send(routed, swap), ring)]
    home_own, *weights = expert(routed, chips, 0, 0, dense, weights, (0,), True)
    done, ready = {}, [home_own, home_own]
    for step in range(1, far):
        passed = []
        for chain in range(2):
            rows = hold(here[chain], ready[chain], *passed)
            passed = [rows]
            if step + 1 < far or chain == 0:
                here[chain] = send(rows, ring)
            if step + 1 < far or chain:
                (done[chain, step],) = expert(rows, chips, step, chain, dense, weights)
                ready[chain] = done[chain, step]
            else:
                late = rows
    (done[0, far],) = expert(hold(here[0], *ready), chips, far, 0, dense, weights)
    if far > 1:
        late = hold(late, done[0, far])
        (done[0, far - 1],) = expert(late, chips, far - 1, 0, dense, weights)

    start = hold(routed, done[0, max(far - 1, 1)])
    (home_other,) = expert(start, chips, 0, 0, dense, weights[3:], (1,))
    moving = [None, None]
    for step in range(far, 0, -1):
        for chain in range(2):
            if (chain, step) in done:
                total = done[chain, step]
                if moving[chain] is not None:
                    total = total + moving[chain]
                moving[chain] = send(total.astype(BF16), back).astype(F32)
    home = mixed + home_own + home_other
    if far > 1:
        home = home + send(moving[1].astype(BF16), swap).astype(F32)
    return (home + moving[0]).astype(BF16)


def solution(mesh):
    rows = P(BOTH, None)
    expert_spec = P("ctx", None, None)
    return jax.shard_map(
        body,
        mesh=mesh,
        in_specs=(rows,) * 4 + (P(),) * 3 + (expert_spec,) * 3 + (rows,) * 2,
        out_specs=rows,
        check_vma=False,
    )
```

```python
import functools

import jax
import jax.numpy as jnp
from jax import lax
from jax.experimental import pallas as pl
from jax.experimental.pallas import tpu as pltpu
from jax.sharding import PartitionSpec as P

HEADS = 8
HEAD = 128
BOTH = ("seg", "ctx")
F32 = jnp.float32
BF16 = jnp.bfloat16
VMEM = pl.BlockSpec(memory_space=pltpu.VMEM)
HBM = pl.BlockSpec(memory_space=pltpu.HBM)
EARLY = 5
LIMIT = 16 * 1024 * 1024


def call(kernel, out_shape, in_specs, flops, *operands):
    many = isinstance(out_shape, list)
    return pl.pallas_call(
        kernel,
        out_shape=out_shape,
        in_specs=in_specs,
        out_specs=[VMEM] * len(out_shape) if many else VMEM,
        compiler_params=pltpu.CompilerParams(vmem_limit_bytes=LIMIT),
        cost_estimate=pl.CostEstimate(flops=flops, bytes_accessed=0, transcendentals=0),
    )(*operands)


def in_hbm(array):
    return pltpu.with_memory_space_constraint(array, pltpu.HBM)


def copies_of(sources, targets, sems):
    copies = [
        pltpu.make_async_copy(source, target, sems.at[i])
        for i, (source, target) in enumerate(zip(sources, targets))
    ]
    for copy in copies:
        copy.start()
    return copies


def chip_order(chips):
    return list(range(0, chips, 2)) + list(range(1, chips, 2))[::-1]


def ring_perm(chips, shift):
    order = chip_order(chips)
    pairs = []
    for place, chip in enumerate(order):
        pairs.append((chip * 2, order[(place + shift) % chips] * 2))
        pairs.append((chip * 2 + 1, order[(place - shift) % chips] * 2 + 1))
    return pairs


def core_perm(chips):
    return [(dev, dev ^ 1) for dev in range(2 * chips)]


def state_kernel(k_hbm, v_hbm, out_ref, k_ref, v_ref, sems):
    for copy in copies_of([k_hbm, v_hbm], [k_ref, v_ref], sems):
        copy.wait()
    for head in range(HEADS):
        cols = pl.ds(head * HEAD, HEAD)
        state = lax.dot_general(
            k_ref[:, cols], v_ref[:, cols], (((0,), (0,)), ((), ())), preferred_element_type=F32
        )
        out_ref[cols, :] = state.astype(BF16)


def inside_kernel(count, *refs):
    q_ref, k_ref, v_ref = refs[count + 1 : count + 4]
    out_hbm, out_ref, sems = refs[2 * count + 1 :]
    copies = copies_of(refs[:count], refs[count + 1 : 2 * count + 1], sems)
    for copy in copies[:3]:
        copy.wait()
    ntok = q_ref.shape[0]
    causal = lax.broadcasted_iota(jnp.int32, (ntok, ntok), 0) >= lax.broadcasted_iota(
        jnp.int32, (ntok, ntok), 1
    )
    for head in range(HEADS):
        cols = pl.ds(head * HEAD, HEAD)
        scores = lax.dot_general(
            q_ref[:, cols], k_ref[:, cols], (((1,), (1,)), ((), ())), preferred_element_type=F32
        )
        scores = jnp.where(causal, scores, 0.0).astype(BF16)
        out_ref[:, cols] = jnp.dot(scores, v_ref[:, cols], preferred_element_type=F32)
    copy = pltpu.make_async_copy(out_ref, out_hbm, sems.at[count])
    copy.start()
    for copy in copies[3:] + [copy]:
        copy.wait()


def attend_inside(arrays, after):
    count = len(arrays)
    outs = [pltpu.VMEM(a.shape, a.dtype) for a in arrays]
    outs.append(pltpu.HBM(arrays[0].shape, F32))
    return pl.pallas_call(
        functools.partial(inside_kernel, count),
        out_shape=outs,
        in_specs=[HBM] * count + [pl.BlockSpec(memory_space=pl.ANY)],
        out_specs=[VMEM] * count + [HBM],
        scratch_shapes=[pltpu.VMEM(arrays[0].shape, F32), pltpu.SemaphoreType.DMA((count + 1,))],
        compiler_params=pltpu.CompilerParams(vmem_limit_bytes=LIMIT),
    )(*[in_hbm(a) for a in arrays], after)


def prefix_kernel(pieces_ref, extra_ref, out_ref):
    devices, share, cols = pieces_ref.shape
    owners = extra_ref.shape[0]
    total = jnp.zeros((share, cols), F32)
    for dev in range(devices):
        rows = jnp.concatenate([total, extra_ref[dev % owners]])
        out_ref[dev] = rows.astype(BF16)
        total += pieces_ref[dev].astype(F32)


def scan_states(states, dense):
    rows, cols = states.shape
    ntok, owners = dense.shape
    devices = lax.axis_size(BOTH)
    share = rows // devices
    top = dense.astype(BF16).astype(F32)
    split = jnp.stack([top.T, (dense - top).T], axis=1)
    pairs = split.reshape(owners // 2, 2, 2, ntok)
    split = jnp.concatenate([split, pairs[:, ::-1].reshape(split.shape)], axis=1)
    extra = split.reshape(owners, 4 * ntok // cols, cols)
    used = extra.shape[1]
    extra = jnp.pad(extra, ((0, 0), (0, -used % 8), (0, 0)))
    pieces = states.reshape(devices, share, cols)
    pieces = lax.all_to_all(pieces, BOTH, split_axis=0, concat_axis=0, tiled=True)
    whole_tiles = share % 16 == 0
    if whole_tiles:
        out = jax.ShapeDtypeStruct((devices, share + extra.shape[1], cols), BF16)
        sums = call(prefix_kernel, out, [VMEM] * 2, 0, pieces, extra)
    else:
        earlier = jnp.arange(devices)[:, None] > jnp.arange(devices)[None, :]
        sums = jnp.dot(
            earlier.astype(BF16),
            pieces.reshape(devices, share * cols),
            preferred_element_type=F32,
        ).reshape(devices, share, cols)
        extra_all = jnp.concatenate([extra] * (devices // owners))
        sums = jnp.concatenate([sums, extra_all], axis=1).astype(BF16)
    sums = lax.all_to_all(sums, BOTH, split_axis=0, concat_axis=0, tiled=True)
    split = lax.dynamic_slice_in_dim(
        sums[:, share : share + used], lax.axis_index("seg") * owners, owners
    )
    split = split.reshape(owners, 4, ntok).astype(F32)
    mine = jnp.concatenate([split[:, 0] + split[:, 1], split[:, 2] + split[:, 3]]).T
    if not whole_tiles:
        sums = sums[:, :share].reshape(rows // HEAD, HEAD, cols)
        share = HEAD
    return sums, share, mine


def rms(rows, gain):
    mean_sq = jnp.mean(rows * rows, axis=1, keepdims=True)
    return rows * lax.rsqrt(mean_sq + 1e-06) * gain


def route_kernel(
    share, sums_ref, q_ref, proj_ref, gain_ref, moe_gain_ref, inside_hbm, hidden_hbm, *refs
):
    mixed_ref, routed_ref, inside_ref, hidden_ref, sems = refs
    copies = copies_of([inside_hbm, hidden_hbm], [inside_ref, hidden_ref], sems)
    ntok, width = q_ref.shape
    slabs = HEAD // share
    attended = []
    for head in range(HEADS):
        cols = pl.ds(head * HEAD, HEAD)
        earlier = jnp.concatenate(
            [sums_ref[head * slabs + i, pl.ds(0, share), :] for i in range(slabs)]
        )
        attended.append(jnp.dot(q_ref[:, cols], earlier, preferred_element_type=F32))
    for copy in copies:
        copy.wait()
    attended = jnp.concatenate(attended, axis=1) + inside_ref[...]
    normed = rms(attended, gain_ref[...]).astype(BF16)
    mixed = hidden_ref[...].astype(F32) + jnp.dot(
        normed, proj_ref[...], preferred_element_type=F32
    )
    mixed_ref[...] = mixed
    routed_ref[...] = rms(mixed, moe_gain_ref[...]).astype(BF16)


def expert_kernel(chips, offset, flip, experts, staged, dense, rows_ref, *refs):
    count = len(refs) - 1 - (len(staged) + 1 if staged else 0)
    weights, out_ref, refs = list(refs[:count]), refs[count], refs[count + 1 :]
    waiting = {}
    if staged:
        copies = copies_of([weights[i] for i in staged], refs[:-1], refs[-1])
        waiting = dict(zip(staged, copies))
        for i, ref in zip(staged, refs):
            weights[i] = ref
    me = lax.axis_index("ctx")
    core, chip = me % 2, me // 2
    place = jnp.where(chip % 2 == 0, chip // 2, chips - 1 - chip // 2)
    spot = (place - (1 - 2 * core) * offset + chips) % chips
    chip = jnp.where(2 * spot < chips, 2 * spot, 2 * (chips - spot) - 1)
    source = chip * 2 + (1 - core if flip else core)
    rows = rows_ref[...]
    table = dense[...]
    lane = lax.broadcasted_iota(jnp.int32, table.shape, 1)
    total = jnp.zeros(rows.shape, F32)
    for i, which in enumerate(experts):
        w_gate, w_up, w_down = weights[3 * i : 3 * i + 3]
        for j in range(3 * i, 3 * i + 3):
            if j in waiting:
                waiting.pop(j).wait()
        gate = jnp.dot(rows, w_gate[0], preferred_element_type=F32)
        upper = jnp.dot(rows, w_up[0], preferred_element_type=F32)
        inner = (gate / (1.0 + jnp.exp(-gate)) * upper).astype(BF16)
        result = jnp.dot(inner, w_down[0], preferred_element_type=F32)
        picked = jnp.where(lane == which * 2 * chips + source, table, 0.0)
        total += result * jnp.sum(picked, axis=1, keepdims=True)
    out_ref[...] = total
    for copy in waiting.values():
        copy.wait()


def expert(rows, chips, offset, flip, dense, weights, experts=(0, 1), staged=()):
    outs = [jax.ShapeDtypeStruct(rows.shape, F32)]
    specs, scratch = [VMEM] * len(weights), []
    if staged:
        outs += [pltpu.VMEM(weights[i].shape, weights[i].dtype) for i in staged]
        specs = [HBM if i in staged else VMEM for i in range(len(weights))]
        weights = [in_hbm(w) if i in staged else w for i, w in enumerate(weights)]
        scratch = [pltpu.SemaphoreType.DMA((len(staged),))]
    return pl.pallas_call(
        functools.partial(expert_kernel, chips, offset, flip, experts, staged),
        out_shape=outs,
        in_specs=[VMEM] * 2 + specs,
        out_specs=[VMEM] * len(outs),
        scratch_shapes=scratch,
        compiler_params=pltpu.CompilerParams(vmem_limit_bytes=LIMIT),
        cost_estimate=pl.CostEstimate(flops=0, bytes_accessed=0, transcendentals=0),
    )(dense, rows, *weights)


def body(
    hidden_in,
    queries,
    key_rows,
    values,
    norm_gain,
    out_proj,
    moe_gain,
    w_gate,
    w_up,
    w_down,
    expert_ids,
    route_scale,
):
    ntok, width = queries.shape
    owners = lax.axis_size("ctx")
    chips = owners // 2
    out = jax.ShapeDtypeStruct((HEADS * HEAD, HEAD), BF16)
    states = pl.pallas_call(
        state_kernel,
        out_shape=out,
        in_specs=[pl.BlockSpec(memory_space=pltpu.HBM)] * 2,
        out_specs=VMEM,
        scratch_shapes=[pltpu.VMEM((ntok, width), BF16)] * 2 + [pltpu.SemaphoreType.DMA((2,))],
        compiler_params=pltpu.CompilerParams(vmem_limit_bytes=LIMIT),
    )(in_hbm(key_rows), in_hbm(values))
    scales = route_scale.astype(F32)
    weight = scales / jnp.sum(scales, axis=1, keepdims=True)
    grid = jnp.arange(owners, dtype=jnp.int32)
    dense = jnp.sum(
        jnp.where(expert_ids[:, :, None] == grid[None, None, :], weight[:, :, None], 0.0), axis=1
    )
    sums, share, dense = scan_states(states, dense)

    out = jax.ShapeDtypeStruct((ntok, width), F32)
    arrays = [queries, key_rows, values, out_proj, norm_gain[None, :], moe_gain[None, :]]
    queries, _, _, out_proj, norm_gain, moe_gain, inside = attend_inside(arrays, states)
    held = [inside, hidden_in]
    mixed, routed = pl.pallas_call(
        functools.partial(route_kernel, share),
        out_shape=[out, jax.ShapeDtypeStruct((ntok, width), BF16)],
        in_specs=[VMEM] * 5 + [HBM] * len(held),
        out_specs=[VMEM] * 2,
        scratch_shapes=[pltpu.VMEM(a.shape, a.dtype) for a in held]
        + [pltpu.SemaphoreType.DMA((len(held),))],
        compiler_params=pltpu.CompilerParams(vmem_limit_bytes=LIMIT),
    )(sums, queries, out_proj, norm_gain, moe_gain, *[in_hbm(a) for a in held])

    far = chips // 2
    ring, back, swap = ring_perm(chips, 1), ring_perm(chips, -1), core_perm(chips)

    def hold(rows, *before):
        return lax.optimization_barrier((rows, before))[0]

    def send(rows, way):
        return lax.ppermute(rows, "ctx", way)

    weights = [w_gate, w_up, w_down]
    weights += [send(w, swap) for w in weights]
    here = [send(routed, ring), send(send(routed, swap), ring)]
    early = tuple(range(EARLY))
    home_own, *held = expert(routed, chips, 0, 0, dense, weights[:EARLY], (0,), early)
    weights = held + weights[EARLY:]
    done, ready = {}, [home_own, home_own]
    for step in range(1, far):
        passed = []
        for chain in range(2):
            rows = hold(here[chain], ready[chain], *passed)
            passed = [rows]
            if step + 1 < far or chain == 0:
                here[chain] = send(rows, ring)
            if step + 1 < far or chain:
                late_ones = () if done else tuple(range(EARLY, 6))
                done[chain, step], *held = expert(
                    rows, chips, step, chain, dense, weights, (0, 1), late_ones
                )
                weights = weights[: len(weights) - len(held)] + held
                ready[chain] = done[chain, step]
            else:
                late = rows
    (done[0, far],) = expert(hold(here[0], *ready), chips, far, 0, dense, weights)
    if far > 1:
        late = hold(late, done[0, far])
        (done[0, far - 1],) = expert(late, chips, far - 1, 0, dense, weights)

    start = hold(routed, done[0, max(far - 1, 1)])
    (home_other,) = expert(start, chips, 0, 0, dense, weights[3:], (1,))
    moving = [None, None]
    for step in range(far, 0, -1):
        for chain in range(2):
            if (chain, step) in done:
                total = done[chain, step]
                if moving[chain] is not None:
                    total = total + moving[chain].astype(F32)
                total = total.astype(BF16)
                moving[chain] = send(total, back)
    home = mixed + home_own + home_other + moving[0].astype(F32)
    if far > 1:
        other = send(moving[1], swap)
        home = home + hold(other, moving[0]).astype(F32)
    return home.astype(BF16)


def solution(mesh):
    rows = P(BOTH, None)
    expert_spec = P("ctx", None, None)
    return jax.shard_map(
        body,
        mesh=mesh,
        in_specs=(rows,) * 4 + (P(),) * 3 + (expert_spec,) * 3 + (rows,) * 2,
        out_specs=rows,
        check_vma=False,
    )
```

```python
import functools

import jax
import jax.numpy as jnp
from jax import lax
from jax.experimental import pallas as pl
from jax.experimental.pallas import tpu as pltpu
from jax.sharding import PartitionSpec as P

HEADS = 8
HEAD = 128
BOTH = ("seg", "ctx")
F32 = jnp.float32
BF16 = jnp.bfloat16
VMEM = pl.BlockSpec(memory_space=pltpu.VMEM)
HBM = pl.BlockSpec(memory_space=pltpu.HBM)
EARLY = 5
LIMIT = 16 * 1024 * 1024


def call(kernel, out_shape, in_specs, flops, *operands):
    many = isinstance(out_shape, list)
    return pl.pallas_call(
        kernel,
        out_shape=out_shape,
        in_specs=in_specs,
        out_specs=[VMEM] * len(out_shape) if many else VMEM,
        compiler_params=pltpu.CompilerParams(vmem_limit_bytes=LIMIT),
        cost_estimate=pl.CostEstimate(flops=flops, bytes_accessed=0, transcendentals=0),
    )(*operands)


def in_hbm(array):
    return pltpu.with_memory_space_constraint(array, pltpu.HBM)


def copies_of(sources, targets, sems):
    copies = [
        pltpu.make_async_copy(source, target, sems.at[i])
        for i, (source, target) in enumerate(zip(sources, targets))
    ]
    for copy in copies:
        copy.start()
    return copies


def chip_order(chips):
    return list(range(0, chips, 2)) + list(range(1, chips, 2))[::-1]


def ring_perm(chips, shift):
    order = chip_order(chips)
    pairs = []
    for place, chip in enumerate(order):
        pairs.append((chip * 2, order[(place + shift) % chips] * 2))
        pairs.append((chip * 2 + 1, order[(place - shift) % chips] * 2 + 1))
    return pairs


def core_perm(chips):
    return [(dev, dev ^ 1) for dev in range(2 * chips)]


def state_kernel(k_hbm, v_hbm, out_ref, k_ref, v_ref, sems):
    for copy in copies_of([k_hbm, v_hbm], [k_ref, v_ref], sems):
        copy.wait()
    for head in range(HEADS):
        cols = pl.ds(head * HEAD, HEAD)
        state = lax.dot_general(
            k_ref[:, cols], v_ref[:, cols], (((0,), (0,)), ((), ())), preferred_element_type=F32
        )
        out_ref[cols, :] = state.astype(BF16)


def inside_kernel(count, *refs):
    q_ref, k_ref, v_ref = refs[count + 1 : count + 4]
    out_hbm, out_ref, sems = refs[2 * count + 1 :]
    copies = copies_of(refs[:count], refs[count + 1 : 2 * count + 1], sems)
    for copy in copies[:3]:
        copy.wait()
    ntok = q_ref.shape[0]
    causal = lax.broadcasted_iota(jnp.int32, (ntok, ntok), 0) >= lax.broadcasted_iota(
        jnp.int32, (ntok, ntok), 1
    )
    for head in range(HEADS):
        cols = pl.ds(head * HEAD, HEAD)
        scores = lax.dot_general(
            q_ref[:, cols], k_ref[:, cols], (((1,), (1,)), ((), ())), preferred_element_type=F32
        )
        scores = jnp.where(causal, scores, 0.0).astype(BF16)
        out_ref[:, cols] = jnp.dot(scores, v_ref[:, cols], preferred_element_type=F32)
    copy = pltpu.make_async_copy(out_ref, out_hbm, sems.at[count])
    copy.start()
    for copy in copies[3:] + [copy]:
        copy.wait()


def attend_inside(arrays, after):
    count = len(arrays)
    outs = [pltpu.VMEM(a.shape, a.dtype) for a in arrays]
    outs.append(pltpu.HBM(arrays[0].shape, F32))
    return pl.pallas_call(
        functools.partial(inside_kernel, count),
        out_shape=outs,
        in_specs=[HBM] * count + [pl.BlockSpec(memory_space=pl.ANY)],
        out_specs=[VMEM] * count + [HBM],
        scratch_shapes=[pltpu.VMEM(arrays[0].shape, F32), pltpu.SemaphoreType.DMA((count + 1,))],
        compiler_params=pltpu.CompilerParams(vmem_limit_bytes=LIMIT),
    )(*[in_hbm(a) for a in arrays], after)


def prefix_kernel(pieces_ref, extra_ref, out_ref):
    devices, share, cols = pieces_ref.shape
    owners = extra_ref.shape[0]
    total = jnp.zeros((share, cols), F32)
    for dev in range(devices):
        rows = jnp.concatenate([total, extra_ref[dev % owners]])
        out_ref[dev] = rows.astype(BF16)
        total += pieces_ref[dev].astype(F32)


def scan_states(states, dense):
    rows, cols = states.shape
    ntok, owners = dense.shape
    devices = lax.axis_size(BOTH)
    share = rows // devices
    top = dense.astype(BF16).astype(F32)
    split = jnp.stack([top.T, (dense - top).T], axis=1)
    pairs = split.reshape(owners // 2, 2, 2, ntok)
    split = jnp.concatenate([split, pairs[:, ::-1].reshape(split.shape)], axis=1)
    extra = split.reshape(owners, 4 * ntok // cols, cols)
    used = extra.shape[1]
    extra = jnp.pad(extra, ((0, 0), (0, -used % 8), (0, 0)))
    pieces = states.reshape(devices, share, cols)
    pieces = lax.all_to_all(pieces, BOTH, split_axis=0, concat_axis=0, tiled=True)
    whole_tiles = share % 16 == 0
    if whole_tiles:
        out = jax.ShapeDtypeStruct((devices, share + extra.shape[1], cols), BF16)
        sums = call(prefix_kernel, out, [VMEM] * 2, 0, pieces, extra)
    else:
        earlier = jnp.arange(devices)[:, None] > jnp.arange(devices)[None, :]
        sums = jnp.dot(
            earlier.astype(BF16),
            pieces.reshape(devices, share * cols),
            preferred_element_type=F32,
        ).reshape(devices, share, cols)
        extra_all = jnp.concatenate([extra] * (devices // owners))
        sums = jnp.concatenate([sums, extra_all], axis=1).astype(BF16)
    sums = lax.all_to_all(sums, BOTH, split_axis=0, concat_axis=0, tiled=True)
    split = lax.dynamic_slice_in_dim(
        sums[:, share : share + used], lax.axis_index("seg") * owners, owners
    )
    split = split.reshape(owners, 4, ntok).astype(F32)
    mine = jnp.concatenate([split[:, 0] + split[:, 1], split[:, 2] + split[:, 3]]).T
    if not whole_tiles:
        sums = sums[:, :share].reshape(rows // HEAD, HEAD, cols)
        share = HEAD
    return sums, share, mine


def rms(rows, gain):
    mean_sq = jnp.mean(rows * rows, axis=1, keepdims=True)
    return rows * lax.rsqrt(mean_sq + 1e-06) * gain


def route_kernel(
    share, sums_ref, q_ref, proj_ref, gain_ref, moe_gain_ref, inside_hbm, hidden_hbm, *refs
):
    mixed_ref, routed_ref, inside_ref, hidden_ref, sems = refs
    copies = copies_of([inside_hbm, hidden_hbm], [inside_ref, hidden_ref], sems)
    ntok, width = q_ref.shape
    slabs = HEAD // share
    attended = []
    for head in range(HEADS):
        cols = pl.ds(head * HEAD, HEAD)
        earlier = jnp.concatenate(
            [sums_ref[head * slabs + i, pl.ds(0, share), :] for i in range(slabs)]
        )
        attended.append(jnp.dot(q_ref[:, cols], earlier, preferred_element_type=F32))
    for copy in copies:
        copy.wait()
    attended = jnp.concatenate(attended, axis=1) + inside_ref[...]
    normed = rms(attended, gain_ref[...]).astype(BF16)
    mixed = hidden_ref[...].astype(F32) + jnp.dot(
        normed, proj_ref[...], preferred_element_type=F32
    )
    mixed_ref[...] = mixed
    routed_ref[...] = rms(mixed, moe_gain_ref[...]).astype(BF16)


def expert_kernel(chips, offset, flip, experts, staged, dense, rows_ref, *refs):
    count = len(refs) - 1 - (len(staged) + 1 if staged else 0)
    weights, out_ref, refs = list(refs[:count]), refs[count], refs[count + 1 :]
    waiting = {}
    if staged:
        copies = copies_of([weights[i] for i in staged], refs[:-1], refs[-1])
        waiting = dict(zip(staged, copies))
        for i, ref in zip(staged, refs):
            weights[i] = ref
    me = lax.axis_index("ctx")
    core, chip = me % 2, me // 2
    place = jnp.where(chip % 2 == 0, chip // 2, chips - 1 - chip // 2)
    spot = (place - (1 - 2 * core) * offset + chips) % chips
    chip = jnp.where(2 * spot < chips, 2 * spot, 2 * (chips - spot) - 1)
    source = chip * 2 + (1 - core if flip else core)
    rows = rows_ref[...]
    table = dense[...]
    lane = lax.broadcasted_iota(jnp.int32, table.shape, 1)
    total = jnp.zeros(rows.shape, F32)
    for i, which in enumerate(experts):
        w_gate, w_up, w_down = weights[3 * i : 3 * i + 3]
        for j in range(3 * i, 3 * i + 3):
            if j in waiting:
                waiting.pop(j).wait()
        gate = jnp.dot(rows, w_gate[0], preferred_element_type=F32)
        upper = jnp.dot(rows, w_up[0], preferred_element_type=F32)
        inner = (gate / (1.0 + jnp.exp(-gate)) * upper).astype(BF16)
        result = jnp.dot(inner, w_down[0], preferred_element_type=F32)
        picked = jnp.where(lane == which * 2 * chips + source, table, 0.0)
        total += result * jnp.sum(picked, axis=1, keepdims=True)
    out_ref[...] = total
    for copy in waiting.values():
        copy.wait()


def expert(rows, chips, offset, flip, dense, weights, experts=(0, 1), staged=()):
    outs = [jax.ShapeDtypeStruct(rows.shape, F32)]
    specs, scratch = [VMEM] * len(weights), []
    if staged:
        outs += [pltpu.VMEM(weights[i].shape, weights[i].dtype) for i in staged]
        specs = [HBM if i in staged else VMEM for i in range(len(weights))]
        weights = [in_hbm(w) if i in staged else w for i, w in enumerate(weights)]
        scratch = [pltpu.SemaphoreType.DMA((len(staged),))]
    return pl.pallas_call(
        functools.partial(expert_kernel, chips, offset, flip, experts, staged),
        out_shape=outs,
        in_specs=[VMEM] * 2 + specs,
        out_specs=[VMEM] * len(outs),
        scratch_shapes=scratch,
        compiler_params=pltpu.CompilerParams(vmem_limit_bytes=LIMIT),
        cost_estimate=pl.CostEstimate(flops=50000000, bytes_accessed=0, transcendentals=0),
    )(dense, rows, *weights)


def body(
    hidden_in,
    queries,
    key_rows,
    values,
    norm_gain,
    out_proj,
    moe_gain,
    w_gate,
    w_up,
    w_down,
    expert_ids,
    route_scale,
):
    ntok, width = queries.shape
    owners = lax.axis_size("ctx")
    chips = owners // 2
    out = jax.ShapeDtypeStruct((HEADS * HEAD, HEAD), BF16)
    states = pl.pallas_call(
        state_kernel,
        out_shape=out,
        in_specs=[pl.BlockSpec(memory_space=pltpu.HBM)] * 2,
        out_specs=VMEM,
        scratch_shapes=[pltpu.VMEM((ntok, width), BF16)] * 2 + [pltpu.SemaphoreType.DMA((2,))],
        compiler_params=pltpu.CompilerParams(vmem_limit_bytes=LIMIT),
    )(in_hbm(key_rows), in_hbm(values))
    scales = route_scale.astype(F32)
    weight = scales / jnp.sum(scales, axis=1, keepdims=True)
    grid = jnp.arange(owners, dtype=jnp.int32)
    dense = jnp.sum(
        jnp.where(expert_ids[:, :, None] == grid[None, None, :], weight[:, :, None], 0.0), axis=1
    )
    sums, share, dense = scan_states(states, dense)

    out = jax.ShapeDtypeStruct((ntok, width), F32)
    arrays = [queries, key_rows, values, out_proj, norm_gain[None, :], moe_gain[None, :]]
    queries, _, _, out_proj, norm_gain, moe_gain, inside = attend_inside(arrays, states)
    held = [inside, hidden_in]
    mixed, routed = pl.pallas_call(
        functools.partial(route_kernel, share),
        out_shape=[out, jax.ShapeDtypeStruct((ntok, width), BF16)],
        in_specs=[VMEM] * 5 + [HBM] * len(held),
        out_specs=[VMEM] * 2,
        scratch_shapes=[pltpu.VMEM(a.shape, a.dtype) for a in held]
        + [pltpu.SemaphoreType.DMA((len(held),))],
        compiler_params=pltpu.CompilerParams(vmem_limit_bytes=LIMIT),
    )(sums, queries, out_proj, norm_gain, moe_gain, *[in_hbm(a) for a in held])

    far = chips // 2
    ring, back, swap = ring_perm(chips, 1), ring_perm(chips, -1), core_perm(chips)

    def hold(rows, *before):
        return lax.optimization_barrier((rows, before))[0]

    def send(rows, way):
        return lax.ppermute(rows, "ctx", way)

    weights = [w_gate, w_up, w_down]
    weights += [send(w, swap) for w in weights]
    here = [send(routed, ring), send(send(routed, swap), ring)]
    early = tuple(range(EARLY))
    home_own, *held = expert(routed, chips, 0, 0, dense, weights[:EARLY], (0,), early)
    weights = held + weights[EARLY:]
    done, ready = {}, [home_own, home_own]
    for step in range(1, far):
        passed = []
        for chain in range(2):
            rows = hold(here[chain], ready[chain], *passed)
            passed = [rows]
            if step + 1 < far or chain == 0:
                here[chain] = send(rows, ring)
            if step + 1 < far or chain:
                late_ones = () if done else tuple(range(EARLY, 6))
                done[chain, step], *held = expert(
                    rows, chips, step, chain, dense, weights, (0, 1), late_ones
                )
                weights = weights[: len(weights) - len(held)] + held
                ready[chain] = done[chain, step]
            else:
                late = rows
    (done[0, far],) = expert(hold(here[0], *ready), chips, far, 0, dense, weights)
    if far > 1:
        late = hold(late, done[0, far])
        (done[0, far - 1],) = expert(late, chips, far - 1, 0, dense, weights)

    start = hold(routed, done[0, max(far - 1, 1)])
    (home_other,) = expert(start, chips, 0, 0, dense, weights[3:], (1,))
    moving = [None, None]
    for step in range(far, 0, -1):
        for chain in range(2):
            if (chain, step) in done:
                total = done[chain, step]
                if moving[chain] is not None:
                    total = total + moving[chain].astype(F32)
                total = total.astype(BF16)
                moving[chain] = send(total, back)
    home = mixed + home_own + home_other + moving[0].astype(F32)
    if far > 1:
        other = send(moving[1], swap)
        home = home + hold(other, moving[0]).astype(F32)
    return home.astype(BF16)


def solution(mesh):
    rows = P(BOTH, None)
    expert_spec = P("ctx", None, None)
    return jax.shard_map(
        body,
        mesh=mesh,
        in_specs=(rows,) * 4 + (P(),) * 3 + (expert_spec,) * 3 + (rows,) * 2,
        out_specs=rows,
        check_vma=False,
    )
```
